512 devices in a mesh: blk: 32 (over x, z_lo), uly: 4 (over y), tp: 4 (over z_hi, core).
Axes of the slice: x: 4, y: 4, z: 16 (z_hi: 2, z_lo: 8; z = z_hi * 8 + z_lo), core: 2. Of those that a mesh axis runs over, the one named last changes fastest.
Arguments:
- query_matrix: bfloat16 [8192, 4, 768], P(('blk', 'uly'), None, 'tp'), may hold values from -16 to 16
- key_matrix: bfloat16 [8192, 384], P(('blk', 'uly')), may hold values from -8 to 8
- value_matrix: bfloat16 [8192, 384], P(('blk', 'uly')), may hold values from -6 to 6
- output_gradient: bfloat16 [8192, 4, 768], P(('blk', 'uly'), None, 'tp'), may hold values from -16 to 16
- stripe_map: int32 [128], replicated, may hold values from 0 to 127, each once
Outputs:
- query_gradients: bfloat16 [8192, 4, 768], P(('blk', 'uly'), None, 'tp')
- key_gradients: bfloat16 [8192, 384], P(('blk', 'uly'), 'tp')
- value_gradients: bfloat16 [8192, 384], P(('blk', 'uly'), 'tp')
The draws below stay inside these ranges and needn't reach their ends.
Inputs may be any that keep to these rules, and one draw needn't show every extreme that they name: `stripe_map`: each of the 128 sequence blocks is held by exactly one stored block.
All inputs are finite; a program needn't handle non-finite values.
Results may differ from the reference program's by a relative error of at most 0.025.
Values may be sent and summed in bfloat16 or wider, within the bound.
A program may use at most 64 MiB of HBM per device.

```python
import jax
import jax.numpy as jnp
from jax import lax

HEAD_WIDTH = 96
KEY_VALUE_HEADS = 4
GROUP_MEMBERS = 8
TOK_DEV = 64
NBLOCKS = 128
SEQUENCE_TOKENS = 8192


def shared_keys(key):
    base_offset = jax.random.normal(key, (SEQUENCE_TOKENS, KEY_VALUE_HEADS * HEAD_WIDTH), jnp.float32) * 1.2
    return jnp.clip(base_offset, -8.0, 8.0)


def draw_key_matrix(key, part):
    field_name = shared_keys(key)
    return field_name.astype(jnp.bfloat16)


def draw_query_matrix(key, part):
    local_key_block = jax.random.fold_in(key, 23)
    local_row_block = jnp.clip(jax.random.normal(local_key_block, (SEQUENCE_TOKENS, KEY_VALUE_HEADS, GROUP_MEMBERS * HEAD_WIDTH), jnp.float32) * 1.2, -8.0, 8.0)
    result = local_row_block
    return result.astype(jnp.bfloat16)


def block_scale(rng, dims, pieces, low, top_value):
    def one(axis_at, shards_of):
        steps = jax.random.uniform(jax.random.fold_in(jax.random.fold_in(rng, 6), axis_at), (shards_of,), jnp.float32, low / len(pieces), top_value / len(pieces))
        return jnp.repeat(jnp.exp(steps), dims[axis_at] // shards_of).reshape((-1,) + (1,) * (len(dims) - axis_at - 1))

    factor_of = one(*pieces[0])
    for cut in pieces[1:]:
        factor_of = factor_of * one(*cut)
    return factor_of


def bell_draw(own_key, dims, deviation, reach, cuts=(), kind=jnp.bfloat16):
    array = deviation * jax.random.normal(own_key, dims, jnp.float32)
    if cuts:
        array = array * block_scale(own_key, dims, cuts, -0.22, 0.18)
    return jnp.clip(array, -reach, reach).astype(kind)


def setup_inputs(seed: int = 0) -> dict:
    key_list = jax.random.split(jax.random.key(seed), 6)
    return {
        "query_matrix": draw_query_matrix(jax.random.fold_in(key_list[5], 71), 0),
        "key_matrix": draw_key_matrix(jax.random.fold_in(key_list[5], 71), 0),
        "value_matrix": bell_draw(key_list[2], (SEQUENCE_TOKENS, KEY_VALUE_HEADS * HEAD_WIDTH), 1.0, 6.0, ((0, 128),)),
        "output_gradient": bell_draw(key_list[3], (SEQUENCE_TOKENS, KEY_VALUE_HEADS, GROUP_MEMBERS * HEAD_WIDTH), 4.0, 16.0, ((0, 128), (2, 4))),
        "stripe_map": jax.random.permutation(key_list[4], NBLOCKS).astype(jnp.int32),
    }


def reference(query_matrix, key_matrix, value_matrix, output_gradient, stripe_map):
    score_scale = HEAD_WIDTH ** -0.5
    row_number = jnp.arange(SEQUENCE_TOKENS, dtype=jnp.int32)
    positions = stripe_map[row_number // TOK_DEV] * TOK_DEV + row_number % TOK_DEV
    visible = positions[None, :] <= positions[:, None]
    total_head_count = KEY_VALUE_HEADS * GROUP_MEMBERS
    query_matrix_view = query_matrix.reshape(SEQUENCE_TOKENS, KEY_VALUE_HEADS, GROUP_MEMBERS, HEAD_WIDTH).transpose(1, 2, 0, 3).reshape(total_head_count, SEQUENCE_TOKENS, HEAD_WIDTH)
    output_gradient_rows = output_gradient.reshape(SEQUENCE_TOKENS, KEY_VALUE_HEADS, GROUP_MEMBERS, HEAD_WIDTH).transpose(1, 2, 0, 3).reshape(total_head_count, SEQUENCE_TOKENS, HEAD_WIDTH)
    every_key_row = key_matrix.reshape(SEQUENCE_TOKENS, KEY_VALUE_HEADS, HEAD_WIDTH).transpose(1, 0, 2)
    every_value_row = value_matrix.reshape(SEQUENCE_TOKENS, KEY_VALUE_HEADS, HEAD_WIDTH).transpose(1, 0, 2)

    def one_head(head_index):
        group_index = head_index // GROUP_MEMBERS
        query_one = query_matrix_view[head_index]
        grad_one = output_gradient_rows[head_index]
        key_one = every_key_row[group_index]
        value_one = every_value_row[group_index]
        scores = jnp.dot(query_one, key_one.T, preferred_element_type=jnp.float32) * score_scale
        masked = jnp.where(visible, scores, -jnp.inf)
        row_max = jnp.max(masked, axis=1, keepdims=True)
        weights = jnp.exp(masked - row_max)
        row_total = jnp.sum(weights, axis=1, keepdims=True)
        output_rows = jnp.dot(weights, value_one.astype(jnp.float32), precision=lax.Precision.HIGHEST, preferred_element_type=jnp.float32) / row_total
        log_total = row_max + jnp.log(row_total)
        probability = jnp.where(visible, jnp.exp(scores - log_total), 0.0)
        value_gradient_part = jnp.dot(probability.astype(jnp.bfloat16).T, grad_one, preferred_element_type=jnp.float32)
        prob_grads = jnp.dot(grad_one, value_one.T, preferred_element_type=jnp.float32)
        output_dot = jnp.sum(grad_one.astype(jnp.float32) * output_rows, axis=1, keepdims=True)
        score_grads = (probability * (prob_grads - output_dot)).astype(jnp.bfloat16)
        query_gradient_part = jnp.dot(score_grads, key_one, preferred_element_type=jnp.float32) * score_scale
        key_gradient_part = jnp.dot(score_grads.T, query_one, preferred_element_type=jnp.float32) * score_scale
        return query_gradient_part, key_gradient_part, value_gradient_part

    query_gradient_part, key_gradient_part, value_gradient_part = lax.map(one_head, jnp.arange(total_head_count, dtype=jnp.int32))
    query_gradients = query_gradient_part.reshape(KEY_VALUE_HEADS, GROUP_MEMBERS, SEQUENCE_TOKENS, HEAD_WIDTH).transpose(2, 0, 1, 3).reshape(SEQUENCE_TOKENS, KEY_VALUE_HEADS, GROUP_MEMBERS * HEAD_WIDTH)
    key_gradients = jnp.sum(key_gradient_part.reshape(KEY_VALUE_HEADS, GROUP_MEMBERS, SEQUENCE_TOKENS, HEAD_WIDTH), axis=1).transpose(1, 0, 2).reshape(SEQUENCE_TOKENS, KEY_VALUE_HEADS * HEAD_WIDTH)
    value_gradients = jnp.sum(value_gradient_part.reshape(KEY_VALUE_HEADS, GROUP_MEMBERS, SEQUENCE_TOKENS, HEAD_WIDTH), axis=1).transpose(1, 0, 2).reshape(SEQUENCE_TOKENS, KEY_VALUE_HEADS * HEAD_WIDTH)
    return query_gradients.astype(jnp.bfloat16), key_gradients.astype(jnp.bfloat16), value_gradients.astype(jnp.bfloat16)
```

```python
import jax
import jax.numpy as jnp
from jax import lax
from jax.experimental import pallas as pl
from jax.experimental.pallas import tpu as pltpu
from jax.sharding import PartitionSpec as P

HEAD = 96
WIDE = 2 * HEAD
TOK = 64
LOG2E = 1.4426950408889634
SCALE = HEAD**-0.5
SCALE2 = SCALE * LOG2E
LOW = -1e30
F32 = jnp.float32
BF16 = jnp.bfloat16
MESH = pl.DeviceIdType.MESH
NT = (((1,), (1,)), ((), ()))
STEPS = (4, 3, -3, 2, -2, 1, -1)
RT = 256


def dot(a, b):
    return jnp.dot(a, b, preferred_element_type=F32)


def kernel(
    stripe, qg, kv, dq_out, dkv_out,
    qga, kva, kvu, kt, wq, wg, prob, grad, stat, stat_in, fac, dqt, dqb, dqr,
    dkf, own, sbs, sbr, l1s, l1r, l2s, l2r,
    loc_sem, kvy_s, kvy_r, qy_s, qy_r, kvz_s, kvz_r, kvs_s, kvs_r, qx_s, qx_r,
    st_s, st_r, sb_s, sb_r, l1_s, l1_r, dq_s, dq_r, l2_s, l2_r,
):
    b, y, t = lax.axis_index("blk"), lax.axis_index("uly"), lax.axis_index("tp")
    x, zl = b // 8, b % 8
    h, c = t // 2, t % 2
    z = h * 8 + zl

    def dev(x_, y_, z_, c_):
        return (x_ * 8 + z_ % 8, y_, (z_ // 8) * 2 + c_)

    def send(src, dst, ss, rs, to):
        copy = pltpu.make_async_remote_copy(
            src_ref=src, dst_ref=dst, send_sem=ss, recv_sem=rs, device_id=to, device_id_type=MESH
        )
        copy.start()
        return copy

    def zstep(k):
        if STEPS[k] == 4:
            return jnp.where(c == 0, 4, 12)
        return STEPS[k] % 16

    barrier = pltpu.get_barrier_semaphore()

    def greet(to):
        pl.semaphore_signal(barrier, inc=1, device_id=to, device_id_type=MESH)

    for i in range(4):
        for j in range(4):
            if i or j:
                greet(dev((x + i) % 4, (y + j) % 4, z, c))
    for d in (-4, -3, -2, -1, 1, 2, 3, 4):
        greet(dev(x, y, (z + d + 16) % 16, c))
    greet(dev(x, y, z, 1 - c))
    mine = (h == y // 2) & (c == y % 2) & (c == y // 2)
    for hs in range(2):
        is_self = mine & (h == hs)

        @pl.when(jnp.logical_not(is_self))
        def _():
            greet(dev(x, t, hs * 8 + zl, y // 2))

    pl.semaphore_wait(barrier, 26 - jnp.where(mine, 1, 0))

    sent = []
    half = pl.ds(pl.multiple_of(16 * c, 16), 16)
    for j in range(1, 4):
        yd = (y + j) % 4
        sent.append(
            send(kv.at[yd, half], kva.at[c, zl, y], kvy_s.at[j], kvy_r.at[j], dev(x, yd, z, c))
        )
    for j in range(1, 4):
        yd = (y + j) % 4
        sent.append(send(qg.at[yd], qga.at[x, y], qy_s.at[j], qy_r.at[j], dev(x, yd, z, c)))
    loc_kv = pltpu.make_async_copy(kv.at[y, half], kva.at[c, zl, y], loc_sem.at[0])
    loc_kv.start()
    loc_qg = pltpu.make_async_copy(qg.at[y], qga.at[x, y], loc_sem.at[1])
    loc_qg.start()
    for i in range(1, 4):
        sent.append(
            send(qg.at[y], qga.at[x, y], qx_s.at[0, i], qx_r.at[i], dev((x + i) % 4, y, z, c))
        )
    loc_kv.wait()
    for j in range(1, 4):
        ys = (y - j + 4) % 4
        pltpu.make_async_copy(kva.at[c, zl, ys], kva.at[c, zl, ys], kvy_r.at[j]).wait()
    for k in range(7):
        sent.append(
            send(
                kva.at[c, zl], kva.at[c, zl], kvz_s.at[k], kvz_r.at[k],
                dev(x, y, (z + zstep(k)) % 16, c),
            )
        )
    sib = dev(x, y, z, 1 - c)
    sent.append(send(kva.at[c, zl], kva.at[c, zl], kvs_s.at[7], kvs_r.at[7], sib))
    for j in range(1, 4):
        ys = (y - j + 4) % 4
        pltpu.make_async_copy(qga.at[x, ys], qga.at[x, ys], qy_r.at[j]).wait()
        for i in range(1, 4):
            sent.append(
                send(
                    qga.at[x, ys], qga.at[x, ys], qx_s.at[j, i], qx_r.at[i],
                    dev((x + i) % 4, y, z, c),
                )
            )
    for k in (5, 6, 3, 4, 1, 2, 0):
        zs = (z - zstep(k) + 16) % 8
        pltpu.make_async_copy(kva.at[c, zs], kva.at[c, zs], kvz_r.at[k]).wait()
        sent.append(send(kva.at[c, zs], kva.at[c, zs], kvs_s.at[k], kvs_r.at[k], sib))
    for k in range(8):
        zs = zl if k == 7 else (z - zstep(k) + 16) % 8
        pltpu.make_async_copy(kva.at[1 - c, zs], kva.at[1 - c, zs], kvs_r.at[k]).wait()

    def unpack(zs, _):
        for ys in range(4):
            for hf in range(2):
                v = kva[hf, zs, ys]
                kvu[zs, TOK * ys + 16 * hf : TOK * ys + 16 * hf + 16, :] = v[:, :WIDE]
                kvu[zs, TOK * ys + 32 + 16 * hf : TOK * ys + 48 + 16 * hf, :] = v[:, WIDE:]
        kt[zs] = jnp.transpose(kvu[zs].astype(F32))[:HEAD].astype(BF16)
        return 0

    lax.fori_loop(0, 8, unpack, 0)

    loc_qg.wait()
    lane = lax.broadcasted_iota(jnp.int32, (1, RT), 1)
    sub = lax.broadcasted_iota(jnp.int32, (TOK, RT), 0)
    low_lanes = lax.broadcasted_iota(jnp.int32, (RT, WIDE), 1) < HEAD

    def rows_pass(xs):
        both = qga[xs].reshape(RT, 2 * WIDE)
        zero = jnp.zeros((RT, WIDE), BF16)
        row_pos = jnp.zeros((1, RT), jnp.int32)
        for ys in range(4):
            first = stripe[(xs * 8 + zl) * 4 + ys] * TOK
            row_pos = jnp.where(lane // TOK == ys, first + lane % TOK, row_pos)
        for m in range(2):
            part = both[:, m * WIDE : (m + 1) * WIDE]
            wq[xs * 2 + m] = jnp.where(low_lanes, part, zero)
            wg[xs * 2 + m] = jnp.where(low_lanes, zero, part)

        def member(m, _):
            rt = xs * 2 + m

            def scores_step(kc, top):
                s = lax.dot_general(kvu[kc], wq[rt], NT, preferred_element_type=F32) * SCALE2
                for ys in range(4):
                    first = stripe[(x * 8 + kc) * 4 + ys] * TOK
                    piece = jnp.where(
                        sub + first <= row_pos, s[TOK * ys : TOK * (ys + 1)], LOW
                    )
                    prob[rt, kc, TOK * ys : TOK * (ys + 1), :] = piece
                    top = jnp.maximum(top, jnp.max(piece.reshape(8, 8, RT), axis=0))
                return top

            top = lax.fori_loop(
                0, 8, scores_step, jnp.full((8, RT), LOW, F32), unroll=8
            )
            top = jnp.max(top, axis=0, keepdims=True)

            def weights_step(kc, sums):
                total, mixed = sums
                pg = lax.dot_general(kvu[kc], wg[rt], NT, preferred_element_type=F32)
                e = jnp.exp2(prob[rt, kc] - top)
                prob[rt, kc] = e
                grad[rt, kc] = pg
                total = total + jnp.sum(e.reshape(32, 8, RT), axis=0)
                mixed = mixed + jnp.sum((e * pg).reshape(32, 8, RT), axis=0)
                return total, mixed

            zero8 = jnp.zeros((8, RT), F32)
            total, mixed = lax.fori_loop(0, 8, weights_step, (zero8, zero8), unroll=8)
            stat[0, pl.ds(rt, 1)] = top
            stat[1, pl.ds(rt, 1)] = jnp.sum(total, axis=0, keepdims=True)
            stat[2, pl.ds(rt, 1)] = jnp.sum(mixed, axis=0, keepdims=True)
            return 0

        lax.fori_loop(0, 2, member, 0)

    rows_pass(x)
    for i in (1, 3, 2):
        xs = (x - i + 4) % 4
        pltpu.make_async_copy(qga.at[xs], qga.at[xs], qx_r.at[i]).wait()
        rows_pass(xs)

    for i in range(1, 4):
        sent.append(
            send(stat, stat_in.at[i], st_s.at[i], st_r.at[i], dev((x + i) % 4, y, z, c))
        )
    dqt[...] = jnp.zeros_like(dqt)
    for i in range(1, 4):
        pltpu.make_async_copy(stat_in.at[i], stat_in.at[i], st_r.at[i]).wait()
    top = stat[0]
    for i in range(1, 4):
        top = jnp.maximum(top, stat_in[i, 0])
    mine_up = jnp.exp2(stat[0] - top)
    total = stat[1] * mine_up
    mixed = stat[2] * mine_up
    for i in range(1, 4):
        up = jnp.exp2(stat_in[i, 0] - top)
        total = total + stat_in[i, 1] * up
        mixed = mixed + stat_in[i, 2] * up
    fac[0] = mine_up / total
    fac[1] = mixed / total

    def give(k):
        pltpu.make_async_copy(sbr.at[k], sbr.at[k], sb_r.at[k]).wait()
        l1s[k] = (own[k] + sbr[k].astype(F32)).astype(BF16)
        sent.append(
            send(
                l1s.at[k], l1r.at[k], l1_s.at[k], l1_r.at[k],
                dev(x, y, (z + zstep(k)) % 16, c),
            )
        )

    for k in range(8):
        kc = zl if k == 7 else (zl + zstep(k)) % 8

        def rows_step(rt, dkv):
            p = prob[rt, kc] * fac[0, pl.ds(rt, 1)]
            ds = (p * (grad[rt, kc] - fac[1, pl.ds(rt, 1)])).astype(BF16)
            dkv = dkv + dot(p.astype(BF16), wg[rt]) + dot(ds, wq[rt])
            dqt[rt] += dot(kt[kc], ds)
            return dkv

        dkf[...] = lax.fori_loop(0, 8, rows_step, jnp.zeros((RT, WIDE), F32), unroll=8)
        sbs[k] = dkf[pl.ds(pl.multiple_of(128 * (1 - c), 128), 128)].astype(BF16)
        own[k] = dkf[pl.ds(pl.multiple_of(128 * c, 128), 128)]
        sent.append(send(sbs.at[k], sbr.at[k], sb_s.at[k], sb_r.at[k], sib))
        if k:
            give(k - 1)

    for i in range(4):
        xs = (x + i) % 4
        pair = dqt[pl.ds(xs * 2, 2)].reshape(WIDE, RT)
        dqb[i] = (jnp.transpose(pair) * SCALE).astype(BF16).reshape(4, TOK, WIDE)
        for j in range(4):
            ys = (y + j) % 4
            if i or j:
                sent.append(
                    send(
                        dqb.at[i, ys], dqr.at[i, y], dq_s.at[i, j], dq_r.at[i, j],
                        dev(xs, ys, z, c),
                    )
                )
            else:
                dqr[0, y] = dqb[0, y]

    pltpu.make_async_copy(sbr.at[7], sbr.at[7], sb_r.at[7]).wait()
    total = own[7] + sbr[7].astype(F32)
    for k in (5, 6, 3, 4, 1, 2, 0):
        pltpu.make_async_copy(l1r.at[k], l1r.at[k], l1_r.at[k]).wait()
        total = total + l1r[k].astype(F32)
    left = lax.broadcasted_iota(jnp.int32, (128, WIDE), 1) < HEAD
    l2s[...] = (total * jnp.where(left, SCALE, 1.0)).astype(BF16).reshape(2, TOK, WIDE)
    for q in range(2):
        yo = 2 * c + q
        is_self = mine & (yo == y)
        to = dev(x, yo, 8 * (y // 2) + zl, y % 2)
        copy = pltpu.make_async_remote_copy(
            src_ref=l2s.at[q], dst_ref=l2r.at[h], send_sem=l2_s.at[q], recv_sem=l2_r.at[h],
            device_id=to, device_id_type=MESH,
        )

        @pl.when(jnp.logical_not(is_self))
        def _():
            copy.start()

        @pl.when(is_self)
        def _():
            l2r[h] = l2s[q]

    for j in range(4):
        gs = (y - j + 4) % 4
        total = jnp.zeros((TOK, WIDE), F32)
        for i in range(4):
            if i or j:
                pltpu.make_async_copy(dqr.at[i, gs], dqr.at[i, gs], dq_r.at[i, j]).wait()
            total = total + dqr[i, gs].astype(F32)
        dq_out[gs] = total.astype(BF16)

    for hs in range(2):
        is_self = mine & (h == hs)

        @pl.when(jnp.logical_not(is_self))
        def _():
            pltpu.make_async_copy(l2r.at[hs], l2r.at[hs], l2_r.at[hs]).wait()

    dkv_out[...] = (l2r[0].astype(F32) + l2r[1].astype(F32)).astype(BF16)
    for copy in sent:
        copy.wait_send()
    for q in range(2):
        is_self = mine & (2 * c + q == y)

        @pl.when(jnp.logical_not(is_self))
        def _():
            pltpu.make_async_copy(l2s.at[q], l2s.at[q], l2_s.at[q]).wait()


def per_device(query_matrix, key_matrix, value_matrix, output_gradient, stripe_map):
    q = query_matrix.reshape(TOK, 4, 2, 1, HEAD)
    g = output_gradient.reshape(TOK, 4, 2, 1, HEAD)
    qg = jnp.concatenate([q, g], axis=3).reshape(TOK, 4, 2 * WIDE).transpose(1, 0, 2)
    k = key_matrix.reshape(2, 32, 4, 1, HEAD)
    v = value_matrix.reshape(2, 32, 4, 1, HEAD)
    kv = jnp.concatenate([k, v], axis=3).transpose(2, 1, 0, 3, 4).reshape(4, 32, 2 * WIDE)
    vmem = pl.BlockSpec(memory_space=pltpu.VMEM)
    dma = pltpu.SemaphoreType.DMA
    dq, dkv = pl.pallas_call(
        kernel,
        out_shape=[
            jax.ShapeDtypeStruct((4, TOK, WIDE), BF16),
            jax.ShapeDtypeStruct((TOK, WIDE), BF16),
        ],
        in_specs=[pl.BlockSpec(memory_space=pltpu.SMEM), vmem, vmem],
        out_specs=[vmem, vmem],
        scratch_shapes=[
            pltpu.VMEM((4, 4, TOK, 2 * WIDE), BF16),
            pltpu.VMEM((2, 8, 4, 16, 2 * WIDE), BF16),
            pltpu.VMEM((8, RT, WIDE), BF16),
            pltpu.VMEM((8, HEAD, RT), BF16),
            pltpu.VMEM((8, RT, WIDE), BF16),
            pltpu.VMEM((8, RT, WIDE), BF16),
            pltpu.VMEM((8, 8, RT, RT), F32),
            pltpu.VMEM((8, 8, RT, RT), F32),
            pltpu.VMEM((3, 8, RT), F32),
            pltpu.VMEM((4, 3, 8, RT), F32),
            pltpu.VMEM((2, 8, RT), F32),
            pltpu.VMEM((8, HEAD, RT), F32),
            pltpu.VMEM((4, 4, TOK, WIDE), BF16),
            pltpu.VMEM((4, 4, TOK, WIDE), BF16),
            pltpu.VMEM((RT, WIDE), F32),
            pltpu.VMEM((8, 128, WIDE), F32),
            pltpu.VMEM((8, 128, WIDE), BF16),
            pltpu.VMEM((8, 128, WIDE), BF16),
            pltpu.VMEM((7, 128, WIDE), BF16),
            pltpu.VMEM((7, 128, WIDE), BF16),
            pltpu.VMEM((2, TOK, WIDE), BF16),
            pltpu.VMEM((2, TOK, WIDE), BF16),
            dma((2,)),
            dma((4,)), dma((4,)), dma((4,)), dma((4,)),
            dma((7,)), dma((7,)), dma((8,)), dma((8,)),
            dma((4, 4)), dma((4,)),
            dma((4,)), dma((4,)), dma((8,)), dma((8,)), dma((7,)), dma((7,)),
            dma((4, 4)), dma((4, 4)), dma((2,)), dma((2,)),
        ],
        compiler_params=pltpu.CompilerParams(
            collective_id=0, has_side_effects=True, vmem_limit_bytes=60 * 2**20
        ),
    )(stripe_map, qg, kv)
    return dq.transpose(1, 0, 2), dkv[:, :HEAD], dkv[:, HEAD:]


def solution(mesh):
    return jax.shard_map(
        per_device,
        mesh=mesh,
        in_specs=(
            P(("blk", "uly"), None, "tp"),
            P(("blk", "uly"), None),
            P(("blk", "uly"), None),
            P(("blk", "uly"), None, "tp"),
            P(),
        ),
        out_specs=(P(("blk", "uly"), None, "tp"), P(("blk", "uly"), "tp"), P(("blk", "uly"), "tp")),
        check_vma=False,
    )
```

```python
import jax
import jax.numpy as jnp
from jax import lax
from jax.experimental import pallas as pl
from jax.experimental.pallas import tpu as pltpu
from jax.sharding import PartitionSpec as P

HEAD = 96
WIDE = 2 * HEAD
TOK = 64
RT = 256
LOG2E = 1.4426950408889634
SCALE = HEAD**-0.5
SCALE2 = SCALE * LOG2E
HIDE = -1e30
FLOOR = -1e29
F32 = jnp.float32
BF16 = jnp.bfloat16
MESH = pl.DeviceIdType.MESH
NT = (((1,), (1,)), ((), ()))
N_SEM = 90


def dot(a, b):
    return jnp.dot(a, b, preferred_element_type=F32)


def kernel(
    stripe, q_in, g_in, k_in, v_in, dq_out, dkv_out,
    qg, kv, qga, kva, kvu, kt, wq, wg, prob, grad,
    tile_top, tile_sum, tile_mix, stat, stat_in, fac, delta,
    dqt, dkf, own, sbs, sbr, l1s, relay, fin, q2s, q2r, q1s, q1r, dqs, l2s, l2r, l2z,
    loc_sem, send_sem, recv_sem, l2_s, l2_r,
):
    b, y, t = lax.axis_index("blk"), lax.axis_index("uly"), lax.axis_index("tp")
    x, zl = b // 8, b % 8
    h, c = t // 2, t % 2
    z = h * 8 + zl

    def dev(x_, y_, z_, c_):
        return (x_ * 8 + z_ % 8, y_, (z_ // 8) * 2 + c_)

    def on_x(i):
        return dev((x + i) % 4, y, z, c)

    def on_y(j):
        return dev(x, (y + j) % 4, z, c)

    def on_z(d):
        return dev(x, y, (z + d) % 16, c)

    sib = dev(x, y, z, 1 - c)
    four = jnp.where(c == 0, 2, 14)
    sent = []
    names = {}

    def send(name, src, dst, to):
        n = names.setdefault(name, len(names))
        copy = pltpu.make_async_remote_copy(
            src_ref=src, dst_ref=dst, send_sem=send_sem.at[n], recv_sem=recv_sem.at[n],
            device_id=to, device_id_type=MESH,
        )
        copy.start()
        sent.append(copy)

    def got(name, ref):
        pltpu.make_async_copy(ref, ref, recv_sem.at[names[name]]).wait()

    barrier = pltpu.get_barrier_semaphore()
    peers = [dev((x + i) % 4, (y + j) % 4, z, c) for i in range(4) for j in range(4) if i or j]
    peers += [on_z(d) for d in (1, 15, 2, 14, 8)]
    peers += [dev(x, (y + j) % 4, z, 1 - c) for j in range(4)]
    for to in peers:
        pl.semaphore_signal(barrier, inc=1, device_id=to, device_id_type=MESH)

    for g in range(4):
        part = slice(g * HEAD, (g + 1) * HEAD)
        kv[g] = jnp.concatenate(
            [k_in[:32, part], v_in[:32, part], k_in[32:, part], v_in[32:, part]], axis=1
        )
        qs, gs = q_in[g], g_in[g]
        qg[g] = jnp.concatenate(
            [qs[:, :HEAD], gs[:, :HEAD], qs[:, HEAD:], gs[:, HEAD:]], axis=1
        )
    pl.semaphore_wait(barrier, len(peers))

    half = pl.ds(pl.multiple_of(16 * c, 16), 16)
    for j in (1, 3, 2):
        send(f"kvy{j}", kv.at[(y + j) % 4, half], kva.at[c, zl, j], on_y(j))
    for d in (1, 15, 2, 14):
        send(f"a{d}", kv.at[y, half], kva.at[c, zl, 0], on_z(d))
    for i in (1, 3):
        send(f"x{i}_0", qg.at[y], qga.at[x, 0], on_x(i))
    for j in (1, 3, 2):
        send(f"qy{j}", qg.at[(y + j) % 4], qga.at[x, j], on_y(j))
    loc_kv = pltpu.make_async_copy(kv.at[y, half], kva.at[c, zl, 0], loc_sem.at[0])
    loc_kv.start()
    loc_qg = pltpu.make_async_copy(qg.at[y], qga.at[x, 0], loc_sem.at[1])
    loc_qg.start()
    rest = pl.ds(1, 3)
    for j in (1, 3, 2):
        got(f"kvy{j}", kva.at[c, zl, j])
    for d in (1, 15, 2, 14):
        send(f"b{d}", kva.at[c, zl, rest], kva.at[c, zl, rest], on_z(d))
    loc_kv.wait()
    send("s0", kva.at[c, zl], kva.at[c, zl], sib)

    def pass_z(part, sl):
        for d in (2, 14):
            zs = (zl + 16 - d) % 8
            got(f"{part}{d}", kva.at[c, zs, sl])
            send(f"{part}3_{d}", kva.at[c, zs, sl], kva.at[c, zs, sl], on_z(1 if d == 2 else 15))
        zs = (zl + 16 - four) % 8
        send(f"{part}4", kva.at[c, zs, sl], kva.at[c, zs, sl], on_z(four))

    def pass_x(j):
        i = 1 if j < 2 else 3
        xs = (x - i + 4) % 4
        got(f"x{i}_{j}", qga.at[xs, j])
        send(f"x2_{j}", qga.at[xs, j], qga.at[xs, j], on_x(i))

    for j in (1, 3, 2):
        got(f"qy{j}", qga.at[x, j])
        for i in (1, 3):
            send(f"x{i}_{j}", qga.at[x, j], qga.at[x, j], on_x(i))
        if j == 1:
            pass_z("a", pl.ds(0, 1))
        if j == 3:
            pass_x(0)

    lane = lax.broadcasted_iota(jnp.int32, (1, RT), 1)
    sub = lax.broadcasted_iota(jnp.int32, (TOK, RT), 0)
    low_lanes = lax.broadcasted_iota(jnp.int32, (RT, WIDE), 1) < HEAD

    def order(n):
        return (zl + jnp.where(n % 2 == 1, (n + 1) // 2, 8 - n // 2)) % 8

    def unpack(n):
        zs = order(n)
        for hf in range(2):
            for j in range(4):
                v = kva[hf, zs, j]
                kvu[zs, TOK * j + 16 * hf : TOK * j + 16 * hf + 16, :] = v[:, :WIDE]
                kvu[zs, TOK * j + 32 + 16 * hf : TOK * j + 48 + 16 * hf, :] = v[:, WIDE:]
        kt[zs] = jnp.transpose(kvu[zs].astype(F32))[:HEAD].astype(BF16)

    def rows_in(xs):
        both = qga[xs].reshape(RT, 2 * WIDE)
        zero = jnp.zeros((RT, WIDE), BF16)
        for m in range(2):
            part = both[:, m * WIDE : (m + 1) * WIDE]
            wq[xs * 2 + m] = jnp.where(low_lanes, part, zero)
            wg[xs * 2 + m] = jnp.where(low_lanes, zero, part)

    def block_of(xs, zs, j):
        return stripe[(xs * 8 + zs) * 4 + (y - j + 4) % 4]

    def rows_of(xs):
        out = jnp.zeros((1, RT), jnp.int32)
        for j in range(4):
            out = jnp.where(lane // TOK == j, block_of(xs, zl, j), out)
        return out

    def tile(xs, row_block, kc, diagonal=False):
        for m in range(2):
            rt = xs * 2 + m
            s = lax.dot_general(kvu[kc], wq[rt], NT, preferred_element_type=F32) * SCALE2
            pg = lax.dot_general(kvu[kc], wg[rt], NT, preferred_element_type=F32)
            pieces, biases = [], []
            top = jnp.full((8, RT), FLOOR, F32)
            for j in range(4):
                piece = s[TOK * j : TOK * (j + 1)]
                key_block = block_of(x, kc, j)
                if diagonal:
                    seen = sub + key_block * TOK <= row_block * TOK + lane % TOK
                    piece = jnp.where(seen, piece, HIDE)
                    bias = jnp.zeros((1, RT), F32)
                else:
                    bias = jnp.where(key_block > row_block, HIDE, 0.0)
                top = jnp.maximum(top, jnp.max(piece.reshape(8, 8, RT), axis=0) + bias)
                pieces.append(piece)
                biases.append(bias)
            top = jnp.max(top, axis=0, keepdims=True)
            total = jnp.zeros((8, RT), F32)
            mixed = jnp.zeros((8, RT), F32)
            for j in range(4):
                e = jnp.exp2(pieces[j] - (top - biases[j]))
                prob[rt, kc, TOK * j : TOK * (j + 1)] = e
                total = total + jnp.sum(e.reshape(8, 8, RT), axis=0)
                mixed = mixed + jnp.sum(
                    (e * pg[TOK * j : TOK * (j + 1)]).reshape(8, 8, RT), axis=0
                )
            grad[rt, kc] = pg
            tile_top[kc, pl.ds(rt, 1)] = top
            tile_sum[kc, pl.ds(rt, 1)] = jnp.sum(total, axis=0, keepdims=True)
            tile_mix[kc, pl.ds(rt, 1)] = jnp.sum(mixed, axis=0, keepdims=True)

    def tiles(xs, lo, hi):
        row_block = rows_of(xs)

        def step(n, _):
            tile(xs, row_block, order(n))
            return 0

        lax.fori_loop(lo, hi, step, 0)

    def unpacks(lo, hi):
        def step(n, _):
            unpack(n)
            return 0

        lax.fori_loop(lo, hi, step, 0)

    loc_qg.wait()
    rows_in(x)
    got("s0", kva.at[1 - c, zl])
    unpack(0)
    tile(x, rows_of(x), zl, True)
    pass_z("b", rest)
    for j in (1, 3, 2):
        pass_x(j)
    for n, d in ((1, 15), (2, 1), (3, 14), (4, 2)):
        zs = order(n)
        if n < 3:
            got(f"a{d}", kva.at[c, zs, pl.ds(0, 1)])
            got(f"b{d}", kva.at[c, zs, rest])
        send(f"s{n}", kva.at[c, zs], kva.at[c, zs], sib)
    for n in range(1, 5):
        got(f"s{n}", kva.at[1 - c, order(n)])
    unpacks(1, 5)
    tiles(x, 1, 5)
    for n, name in ((5, "3_14"), (6, "3_2"), (7, "4")):
        zs = order(n)
        got("a" + name, kva.at[c, zs, pl.ds(0, 1)])
        got("b" + name, kva.at[c, zs, rest])
        send(f"s{n}", kva.at[c, zs], kva.at[c, zs], sib)
    for i in (1, 3):
        xs = (x - i + 4) % 4
        for j in (2, 3) if i == 1 else (0, 1):
            got(f"x{i}_{j}", qga.at[xs, j])
        rows_in(xs)
        tiles(xs, 0, 5)
    for n in range(5, 8):
        got(f"s{n}", kva.at[1 - c, order(n)])
    unpacks(5, 8)

    def late(i, _):
        tiles((x + i + i // 2) % 4, 5, 8)
        return 0

    lax.fori_loop(0, 3, late, 0)
    xs = (x + 2) % 4
    for j in range(4):
        got(f"x2_{j}", qga.at[xs, j])
    rows_in(xs)
    tiles(xs, 0, 8)

    top = tile_top[0]
    for kc in range(1, 8):
        top = jnp.maximum(top, tile_top[kc])
    total = jnp.zeros((8, RT), F32)
    mixed = jnp.zeros((8, RT), F32)
    for kc in range(8):
        up = jnp.exp2(tile_top[kc] - top)
        total = total + tile_sum[kc] * up
        mixed = mixed + tile_mix[kc] * up
    stat[0] = top
    stat[1] = total
    stat[2] = mixed
    for i in (2, 1, 3):
        send(f"st{i}", stat, stat_in.at[i], on_x(i))
    dqt[...] = jnp.zeros_like(dqt)
    for i in (1, 3, 2):
        got(f"st{i}", stat_in.at[i])
    all_top = top
    for i in range(1, 4):
        all_top = jnp.maximum(all_top, stat_in[i, 0])
    up = jnp.exp2(top - all_top)
    total = total * up
    mixed = mixed * up
    for i in range(1, 4):
        up = jnp.exp2(stat_in[i, 0] - all_top)
        total = total + stat_in[i, 1] * up
        mixed = mixed + stat_in[i, 2] * up
    inverse = 1.0 / total
    delta[...] = mixed * inverse
    for kc in range(8):
        fac[kc] = jnp.exp2(tile_top[kc] - all_top) * inverse

    steps = (4, 3, 13, 2, 14, 1, 15, 0)

    def give(k):
        got(f"sb{k}", sbr.at[k])
        total = own[k] + sbr[k].astype(F32)
        if k == 3:
            got("r3", relay.at[0])
            got("r13", relay.at[1])
            got("r4", relay.at[2])
        if k in (3, 4):
            total = total + relay[k - 3].astype(F32)
            far = relay[2].astype(F32)
            total = total + jnp.where(c == k - 3, far, jnp.zeros_like(far))
        l1s[k] = total.astype(BF16)
        if k == 0:
            send("r4", l1s.at[k], relay.at[2], on_z(four))
        elif k < 3:
            send(f"r{steps[k]}", l1s.at[k], relay.at[k - 1], on_z(1 if k == 1 else 15))
        else:
            send(f"f{steps[k]}", l1s.at[k], fin.at[k - 3], on_z(steps[k]))

    for k in range(8):
        kc = (zl + steps[k]) % 8

        def rows_step(rt, dkv):
            p = prob[rt, kc] * fac[kc, pl.ds(rt, 1)]
            ds = (p * (grad[rt, kc] - delta[pl.ds(rt, 1)])).astype(BF16)
            dkv = dkv + dot(p.astype(BF16), wg[rt]) + dot(ds, wq[rt])
            dqt[rt] += dot(kt[kc], ds)
            return dkv

        dkf[...] = lax.fori_loop(0, 8, rows_step, jnp.zeros((RT, WIDE), F32), unroll=8)
        sbs[k] = dkf[pl.ds(pl.multiple_of(128 * (1 - c), 128), 128)].astype(BF16)
        own[k] = dkf[pl.ds(pl.multiple_of(128 * c, 128), 128)]
        send(f"sb{k}", sbs.at[k], sbr.at[k], sib)
        if k >= 2 and k < 7:
            give(k - 2)

    def rows_out(i):
        xs = (x + i) % 4
        pair = dqt[pl.ds(xs * 2, 2)].reshape(WIDE, RT)
        return (jnp.transpose(pair) * SCALE).reshape(4, TOK, WIDE)

    q2s[...] = rows_out(2).astype(BF16)
    send("q2p", q2s.at[pl.ds(0, 2)], q2r.at[0], on_x(1))
    send("q2m", q2s.at[pl.ds(2, 2)], q2r.at[1], on_x(3))
    give(5)
    ahead, back = rows_out(1), rows_out(3)
    q1s[0, 2:] = ahead[2:].astype(BF16)
    q1s[1, :2] = back[:2].astype(BF16)
    send("q1pb", q1s.at[0, pl.ds(2, 2)], q1r.at[0, pl.ds(2, 2)], on_x(1))
    send("q1ma", q1s.at[1, pl.ds(0, 2)], q1r.at[1, pl.ds(0, 2)], on_x(3))
    give(6)
    got("q2p", q2r.at[0])
    q1s[0, :2] = (ahead[:2] + q2r[0].astype(F32)).astype(BF16)
    send("q1pa", q1s.at[0, pl.ds(0, 2)], q1r.at[0, pl.ds(0, 2)], on_x(1))
    got("q2m", q2r.at[1])
    q1s[1, 2:] = (back[2:] + q2r[1].astype(F32)).astype(BF16)
    send("q1mb", q1s.at[1, pl.ds(2, 2)], q1r.at[1, pl.ds(2, 2)], on_x(3))
    mid = rows_out(0)

    got("sb7", sbr.at[7])
    total = own[7] + sbr[7].astype(F32)
    for k in range(3, 7):
        got(f"f{steps[k]}", fin.at[k - 3])
        total = total + fin[k - 3].astype(F32)
    left = lax.broadcasted_iota(jnp.int32, (128, WIDE), 1) < HEAD
    l2s[...] = (total * jnp.where(left, SCALE, 1.0)).astype(BF16).reshape(2, TOK, WIDE)
    head_pair = y // 2
    for q in range(2):
        j = 2 * c + q
        is_self = (c == 0) & (y % 2 == 0) & (q == 0)
        copy = pltpu.make_async_remote_copy(
            src_ref=l2s.at[q], dst_ref=l2r.at[head_pair],
            send_sem=l2_s.at[q], recv_sem=l2_r.at[head_pair],
            device_id=dev(x, (y - j + 4) % 4, z, y % 2), device_id_type=MESH,
        )

        @pl.when(jnp.logical_not(is_self))
        def _():
            copy.start()

        @pl.when(is_self)
        def _():
            l2r[head_pair] = l2s[q]

    got("q1pb", q1r.at[0, pl.ds(2, 2)])
    got("q1ma", q1r.at[1, pl.ds(0, 2)])
    got("q1pa", q1r.at[0, pl.ds(0, 2)])
    got("q1mb", q1r.at[1, pl.ds(2, 2)])
    mid = mid + q1r[0].astype(F32) + q1r[1].astype(F32)
    dqs[...] = mid.astype(BF16)
    for j in (2, 1, 3):
        send(f"dq{j}", dqs.at[j], dq_out.at[y], on_y(4 - j))
    dq_out[y] = dqs[0]

    for hs in range(2):
        is_self = (c == 0) & (y % 2 == 0) & (head_pair == hs)

        @pl.when(jnp.logical_not(is_self))
        def _():
            pltpu.make_async_copy(l2r.at[hs], l2r.at[hs], l2_r.at[hs]).wait()

    send("zz", l2r.at[1 - h], l2z, on_z(8))
    for j in (1, 3, 2):
        got(f"dq{j}", dq_out.at[(y + j) % 4])
    got("zz", l2z)
    dkv_out[...] = (l2r[h].astype(F32) + l2z[...].astype(F32)).astype(BF16)
    for copy in sent:
        copy.wait_send()
    for q in range(2):
        is_self = (c == 0) & (y % 2 == 0) & (q == 0)

        @pl.when(jnp.logical_not(is_self))
        def _():
            pltpu.make_async_copy(l2s.at[q], l2s.at[q], l2_s.at[q]).wait()


def per_device(query_matrix, key_matrix, value_matrix, output_gradient, stripe_map):
    vmem = pl.BlockSpec(memory_space=pltpu.VMEM)
    dma = pltpu.SemaphoreType.DMA
    dq, dkv = pl.pallas_call(
        kernel,
        out_shape=[
            jax.ShapeDtypeStruct((4, TOK, WIDE), BF16),
            jax.ShapeDtypeStruct((TOK, WIDE), BF16),
        ],
        in_specs=[pl.BlockSpec(memory_space=pltpu.SMEM)] + [vmem] * 4,
        out_specs=[vmem, vmem],
        scratch_shapes=[
            pltpu.VMEM((4, TOK, 2 * WIDE), BF16),
            pltpu.VMEM((4, 32, 2 * WIDE), BF16),
            pltpu.VMEM((4, 4, TOK, 2 * WIDE), BF16),
            pltpu.VMEM((2, 8, 4, 16, 2 * WIDE), BF16),
            pltpu.VMEM((8, RT, WIDE), BF16),
            pltpu.VMEM((8, HEAD, RT), BF16),
            pltpu.VMEM((8, RT, WIDE), BF16),
            pltpu.VMEM((8, RT, WIDE), BF16),
            pltpu.VMEM((8, 8, RT, RT), F32),
            pltpu.VMEM((8, 8, RT, RT), F32),
            pltpu.VMEM((8, 8, RT), F32),
            pltpu.VMEM((8, 8, RT), F32),
            pltpu.VMEM((8, 8, RT), F32),
            pltpu.VMEM((3, 8, RT), F32),
            pltpu.VMEM((4, 3, 8, RT), F32),
            pltpu.VMEM((8, 8, RT), F32),
            pltpu.VMEM((8, RT), F32),
            pltpu.VMEM((8, HEAD, RT), F32),
            pltpu.VMEM((RT, WIDE), F32),
            pltpu.VMEM((8, 128, WIDE), F32),
            pltpu.VMEM((8, 128, WIDE), BF16),
            pltpu.VMEM((8, 128, WIDE), BF16),
            pltpu.VMEM((7, 128, WIDE), BF16),
            pltpu.VMEM((3, 128, WIDE), BF16),
            pltpu.VMEM((4, 128, WIDE), BF16),
            pltpu.VMEM((4, TOK, WIDE), BF16),
            pltpu.VMEM((2, 2, TOK, WIDE), BF16),
            pltpu.VMEM((2, 4, TOK, WIDE), BF16),
            pltpu.VMEM((2, 4, TOK, WIDE), BF16),
            pltpu.VMEM((4, TOK, WIDE), BF16),
            pltpu.VMEM((2, TOK, WIDE), BF16),
            pltpu.VMEM((2, TOK, WIDE), BF16),
            pltpu.VMEM((TOK, WIDE), BF16),
            dma((2,)), dma((N_SEM,)), dma((N_SEM,)), dma((2,)), dma((2,)),
        ],
        compiler_params=pltpu.CompilerParams(
            collective_id=0, has_side_effects=True, vmem_limit_bytes=50 * 2**20
        ),
    )(
        stripe_map,
        query_matrix.transpose(1, 0, 2),
        output_gradient.transpose(1, 0, 2),
        key_matrix,
        value_matrix,
    )
    return dq.transpose(1, 0, 2), dkv[:, :HEAD], dkv[:, HEAD:]


def solution(mesh):
    return jax.shard_map(
        per_device,
        mesh=mesh,
        in_specs=(
            P(("blk", "uly"), None, "tp"),
            P(("blk", "uly"), None),
            P(("blk", "uly"), None),
            P(("blk", "uly"), None, "tp"),
            P(),
        ),
        out_specs=(P(("blk", "uly"), None, "tp"), P(("blk", "uly"), "tp"), P(("blk", "uly"), "tp")),
        check_vma=False,
    )
```

```python
import jax
import jax.numpy as jnp
from jax import lax
from jax.experimental import pallas as pl
from jax.experimental.pallas import tpu as pltpu
from jax.sharding import PartitionSpec as P

HEAD = 96
WIDE = 2 * HEAD
TOK = 64
RT = 256
LOG2E = 1.4426950408889634
SCALE = HEAD**-0.5
SCALE2 = SCALE * LOG2E
HIDE = -1e30
FLOOR = -1e29
F32 = jnp.float32
BF16 = jnp.bfloat16
MESH = pl.DeviceIdType.MESH
NT = (((1,), (1,)), ((), ()))
N_SEM = 96


def dot(a, b):
    return jnp.dot(a, b, preferred_element_type=F32)


def kernel(
    stripe, q_in, g_in, k_in, v_in, dq_out, dkv_out,
    qg, kv, qga, kva, kvu, kt, wq, wg, prob, grad,
    tile_top, tile_sum, tile_mix, stat, stat_in, fac, delta,
    dqt, dkf, own, sbs, sbr, l1s, fin, dqb, dqr, l2s, l2r,
    loc_sem, send_sem, recv_sem, l2_s, l2_r,
):
    b, y, t = lax.axis_index("blk"), lax.axis_index("uly"), lax.axis_index("tp")
    x, zl = b // 8, b % 8
    h, c = t // 2, t % 2
    z = h * 8 + zl

    def dev(x_, y_, z_, c_):
        return (x_ * 8 + z_ % 8, y_, (z_ // 8) * 2 + c_)

    def on_x(i):
        return dev((x + i) % 4, y, z, c)

    def on_y(j):
        return dev(x, (y + j) % 4, z, c)

    def on_z(d):
        return dev(x, y, (z + d) % 16, c)

    sib = dev(x, y, z, 1 - c)
    zsteps = (0, 1, 15, 2, 14, 3, 13, jnp.where(c == 0, 4, 12))
    sent = []
    names = {}

    def send(name, src, dst, to):
        n = names.setdefault(name, len(names))
        copy = pltpu.make_async_remote_copy(
            src_ref=src, dst_ref=dst, send_sem=send_sem.at[n], recv_sem=recv_sem.at[n],
            device_id=to, device_id_type=MESH,
        )
        copy.start()
        sent.append(copy)

    def got(name, ref):
        pltpu.make_async_copy(ref, ref, recv_sem.at[names[name]]).wait()

    barrier = pltpu.get_barrier_semaphore()
    peers = [dev((x + i) % 4, (y + j) % 4, z, c) for i in range(4) for j in range(4) if i or j]
    peers += [
        dev(x, (y + j) % 4, (z + d) % 16, c) for d in (1, 15, 2, 14, 3, 13, 4, 12) for j in range(4)
    ]
    peers += [sib]

    def greet(to):
        pl.semaphore_signal(barrier, inc=1, device_id=to, device_id_type=MESH)

    for to in peers:
        greet(to)
    mine = (c == 0) & (y % 2 == 0) & (h == y // 2)
    for hs in range(2):

        @pl.when(jnp.logical_not(mine & (h == hs)))
        def _():
            greet(dev(x, t, hs * 8 + zl, ((t - y + 4) % 4) // 2))

    for g in range(4):
        part = slice(g * HEAD, (g + 1) * HEAD)
        kv[g] = jnp.concatenate(
            [k_in[:32, part], v_in[:32, part], k_in[32:, part], v_in[32:, part]], axis=1
        )
        qs, gs = q_in[g], g_in[g]
        qg[g] = jnp.concatenate(
            [qs[:, :HEAD], gs[:, :HEAD], qs[:, HEAD:], gs[:, HEAD:]], axis=1
        )
    pl.semaphore_wait(barrier, len(peers) + 2 - jnp.where(mine, 1, 0))

    half = pl.ds(pl.multiple_of(16 * c, 16), 16)

    def send_kv(n, j):
        send(
            f"k{n}_{j}", kv.at[(y + j) % 4, half], kva.at[c, zl, j],
            dev(x, (y + j) % 4, (z + zsteps[n]) % 16, c),
        )

    loc_kv = pltpu.make_async_copy(kv.at[y, half], kva.at[c, zl, 0], loc_sem.at[0])
    loc_kv.start()
    loc_qg = pltpu.make_async_copy(qg.at[y], qga.at[x, 0], loc_sem.at[1])
    loc_qg.start()
    for j in (1, 3, 2):
        send_kv(0, j)
    for j in (1, 3, 2):
        send(f"qy{j}", qg.at[(y + j) % 4], qga.at[x, j], on_y(j))
    for i in (1, 3, 2):
        send(f"x{i}_0", qg.at[y], qga.at[x, 0], on_x(i))
    for n in range(1, 8):
        for j in (0, 1, 3, 2):
            send_kv(n, j)

    def share_kv(n):
        zs = (zl + 16 - zsteps[n]) % 8
        for j in range(4):
            if n or j:
                got(f"k{n}_{j}", kva.at[c, zs, j])
        send(f"s{n}", kva.at[c, zs], kva.at[c, zs], sib)

    loc_kv.wait()
    share_kv(0)
    for j in (1, 3, 2):
        got(f"qy{j}", qga.at[x, j])
        for i in (1, 3):
            send(f"x{i}_{j}", qga.at[x, j], qga.at[x, j], on_x(i))
    for j in (1, 3, 2):
        send(f"x2_{j}", qga.at[x, j], qga.at[x, j], on_x(2))

    lane = lax.broadcasted_iota(jnp.int32, (1, RT), 1)
    sub = lax.broadcasted_iota(jnp.int32, (TOK, RT), 0)
    low_lanes = lax.broadcasted_iota(jnp.int32, (RT, WIDE), 1) < HEAD

    def order(n):
        return (zl + jnp.where(n % 2 == 1, 8 - (n + 1) // 2, n // 2)) % 8

    def unpack(n):
        zs = order(n)
        for hf in range(2):
            for j in range(4):
                v = kva[hf, zs, j]
                kvu[zs, TOK * j + 16 * hf : TOK * j + 16 * hf + 16, :] = v[:, :WIDE]
                kvu[zs, TOK * j + 32 + 16 * hf : TOK * j + 48 + 16 * hf, :] = v[:, WIDE:]

    def rows_in(xs):
        both = qga[xs].reshape(RT, 2 * WIDE)
        zero = jnp.zeros((RT, WIDE), BF16)
        for m in range(2):
            part = both[:, m * WIDE : (m + 1) * WIDE]
            wq[xs * 2 + m] = jnp.where(low_lanes, part, zero)
            wg[xs * 2 + m] = jnp.where(low_lanes, zero, part)

    def block_of(xs, zs, j):
        return stripe[(xs * 8 + zs) * 4 + (y - j + 4) % 4]

    def rows_of(xs):
        out = jnp.zeros((1, RT), jnp.int32)
        for j in range(4):
            out = jnp.where(lane // TOK == j, block_of(xs, zl, j), out)
        return out

    def tile(xs, row_block, kc, diagonal=False):
        for m in range(2):
            rt = xs * 2 + m
            s = lax.dot_general(kvu[kc], wq[rt], NT, preferred_element_type=F32) * SCALE2
            pg = lax.dot_general(kvu[kc], wg[rt], NT, preferred_element_type=F32)
            pieces, biases = [], []
            top = jnp.full((8, RT), FLOOR, F32)
            for j in range(4):
                piece = s[TOK * j : TOK * (j + 1)]
                key_block = block_of(x, kc, j)
                if diagonal:
                    seen = sub + key_block * TOK <= row_block * TOK + lane % TOK
                    piece = jnp.where(seen, piece, HIDE)
                    bias = jnp.zeros((1, RT), F32)
                else:
                    bias = jnp.where(key_block > row_block, HIDE, 0.0)
                top = jnp.maximum(top, jnp.max(piece.reshape(8, 8, RT), axis=0) + bias)
                pieces.append(piece)
                biases.append(bias)
            top = jnp.max(top, axis=0, keepdims=True)
            total = jnp.zeros((8, RT), F32)
            mixed = jnp.zeros((8, RT), F32)
            for j in range(4):
                e = jnp.exp2(pieces[j] - (top - biases[j]))
                prob[rt, kc, TOK * j : TOK * (j + 1)] = e
                total = total + jnp.sum(e.reshape(8, 8, RT), axis=0)
                mixed = mixed + jnp.sum(
                    (e * pg[TOK * j : TOK * (j + 1)]).reshape(8, 8, RT), axis=0
                )
            grad[rt, kc] = pg
            tile_top[kc, pl.ds(rt, 1)] = top
            tile_sum[kc, pl.ds(rt, 1)] = jnp.sum(total, axis=0, keepdims=True)
            tile_mix[kc, pl.ds(rt, 1)] = jnp.sum(mixed, axis=0, keepdims=True)

    def tiles(xs, lo, count, turns=1):
        row_block = rows_of(xs)

        def step(turn, _):
            for n in range(count):
                tile(xs, row_block, order(lo + turn * count + n))
            return 0

        lax.fori_loop(0, turns, step, 0)

    loc_qg.wait()
    rows_in(x)
    got("s0", kva.at[1 - c, zl])
    unpack(0)
    tile(x, rows_of(x), zl, True)
    for lo, count in ((1, 4), (5, 3)):
        for n in range(lo, lo + count):
            share_kv(n)
        for n in range(lo, lo + count):
            got(f"s{n}", kva.at[1 - c, order(n)])
            unpack(n)
        tiles(x, lo, count)
    for i in (1, 3, 2):
        xs = (x - i + 4) % 4
        for j in range(4):
            got(f"x{i}_{j}", qga.at[xs, j])
        rows_in(xs)
        tiles(xs, 0, 4, 2)

    top = tile_top[0]
    for kc in range(1, 8):
        top = jnp.maximum(top, tile_top[kc])
    total = jnp.zeros((8, RT), F32)
    mixed = jnp.zeros((8, RT), F32)
    for kc in range(8):
        up = jnp.exp2(tile_top[kc] - top)
        total = total + tile_sum[kc] * up
        mixed = mixed + tile_mix[kc] * up
    stat[0] = top
    stat[1] = total
    stat[2] = mixed
    for i in (2, 1, 3):
        send(f"st{i}", stat, stat_in.at[i], on_x(i))
    dqt[...] = jnp.zeros_like(dqt)

    def turn_keys(kc, _):
        kt[kc] = jnp.transpose(kvu[kc].astype(F32))[:HEAD].astype(BF16)
        return 0

    lax.fori_loop(0, 8, turn_keys, 0)
    for i in (1, 3, 2):
        got(f"st{i}", stat_in.at[i])
    all_top = top
    for i in range(1, 4):
        all_top = jnp.maximum(all_top, stat_in[i, 0])
    up = jnp.exp2(top - all_top)
    total = total * up
    mixed = mixed * up
    for i in range(1, 4):
        up = jnp.exp2(stat_in[i, 0] - all_top)
        total = total + stat_in[i, 1] * up
        mixed = mixed + stat_in[i, 2] * up
    inverse = 1.0 / total
    delta[...] = mixed * inverse
    for kc in range(8):
        fac[kc] = jnp.exp2(tile_top[kc] - all_top) * inverse

    steps = (zsteps[7], 3, 13, 2, 14, 1, 15, 0)

    def give(k):
        got(f"sb{k}", sbr.at[k])
        l1s[k] = (own[k] + sbr[k].astype(F32)).astype(BF16)
        send(f"f{k}", l1s.at[k], fin.at[k], on_z(steps[k]))

    for k in range(8):
        kc = (zl + steps[k]) % 8

        def rows_step(rt, dkv):
            p = prob[rt, kc] * fac[kc, pl.ds(rt, 1)]
            ds = (p * (grad[rt, kc] - delta[pl.ds(rt, 1)])).astype(BF16)
            dkv = dkv + dot(p.astype(BF16), wg[rt]) + dot(ds, wq[rt])
            dqt[rt] += dot(kt[kc], ds)
            return dkv

        dkf[...] = lax.fori_loop(0, 8, rows_step, jnp.zeros((RT, WIDE), F32), unroll=8)
        sbs[k] = dkf[pl.ds(pl.multiple_of(128 * (1 - c), 128), 128)].astype(BF16)
        own[k] = dkf[pl.ds(pl.multiple_of(128 * c, 128), 128)]
        send(f"sb{k}", sbs.at[k], sbr.at[k], sib)
        if k >= 2 and k < 7:
            give(k - 2)

    give(5)
    for i in (2, 1, 3, 0):
        xs = (x + i) % 4
        pair = dqt[pl.ds(xs * 2, 2)].reshape(WIDE, RT)
        dqb[i] = (jnp.transpose(pair) * SCALE).astype(BF16).reshape(4, TOK, WIDE)
        for j in (2, 1, 3, 0):
            if i or j:
                send(
                    f"dq{i}_{j}", dqb.at[i, j], dqr.at[i, y],
                    dev(xs, (y - j + 4) % 4, z, c),
                )
        if i == 2:
            give(6)
    dqr[0, y] = dqb[0, 0]

    got("sb7", sbr.at[7])
    total = own[7] + sbr[7].astype(F32)
    for k in range(7):
        got(f"f{k}", fin.at[k])
        total = total + fin[k].astype(F32)
    left = lax.broadcasted_iota(jnp.int32, (128, WIDE), 1) < HEAD
    l2s[...] = (total * jnp.where(left, SCALE, 1.0)).astype(BF16).reshape(2, TOK, WIDE)
    for q in range(2):
        j = 2 * c + q
        yo = (y - j + 4) % 4
        is_self = mine & (yo == y)
        copy = pltpu.make_async_remote_copy(
            src_ref=l2s.at[q], dst_ref=l2r.at[h], send_sem=l2_s.at[q], recv_sem=l2_r.at[h],
            device_id=dev(x, yo, 8 * (y // 2) + zl, y % 2), device_id_type=MESH,
        )

        @pl.when(jnp.logical_not(is_self))
        def _():
            copy.start()

        @pl.when(is_self)
        def _():
            l2r[h] = l2s[q]

    for j in range(4):
        gs = (y + j) % 4
        total = jnp.zeros((TOK, WIDE), F32)
        for i in (0, 1, 3, 2):
            if i or j:
                got(f"dq{i}_{j}", dqr.at[i, gs])
            total = total + dqr[i, gs].astype(F32)
        dq_out[gs] = total.astype(BF16)

    for hs in range(2):

        @pl.when(jnp.logical_not(mine & (h == hs)))
        def _():
            pltpu.make_async_copy(l2r.at[hs], l2r.at[hs], l2_r.at[hs]).wait()

    dkv_out[...] = (l2r[0].astype(F32) + l2r[1].astype(F32)).astype(BF16)
    for copy in sent:
        copy.wait_send()
    for q in range(2):
        yo = (y - 2 * c - q + 4) % 4

        @pl.when(jnp.logical_not(mine & (yo == y)))
        def _():
            pltpu.make_async_copy(l2s.at[q], l2s.at[q], l2_s.at[q]).wait()


def per_device(query_matrix, key_matrix, value_matrix, output_gradient, stripe_map):
    vmem = pl.BlockSpec(memory_space=pltpu.VMEM)
    dma = pltpu.SemaphoreType.DMA
    dq, dkv = pl.pallas_call(
        kernel,
        out_shape=[
            jax.ShapeDtypeStruct((4, TOK, WIDE), BF16),
            jax.ShapeDtypeStruct((TOK, WIDE), BF16),
        ],
        in_specs=[pl.BlockSpec(memory_space=pltpu.SMEM)] + [vmem] * 4,
        out_specs=[vmem, vmem],
        scratch_shapes=[
            pltpu.VMEM((4, TOK, 2 * WIDE), BF16),
            pltpu.VMEM((4, 32, 2 * WIDE), BF16),
            pltpu.VMEM((4, 4, TOK, 2 * WIDE), BF16),
            pltpu.VMEM((2, 8, 4, 16, 2 * WIDE), BF16),
            pltpu.VMEM((8, RT, WIDE), BF16),
            pltpu.VMEM((8, HEAD, RT), BF16),
            pltpu.VMEM((8, RT, WIDE), BF16),
            pltpu.VMEM((8, RT, WIDE), BF16),
            pltpu.VMEM((8, 8, RT, RT), F32),
            pltpu.VMEM((8, 8, RT, RT), F32),
            pltpu.VMEM((8, 8, RT), F32),
            pltpu.VMEM((8, 8, RT), F32),
            pltpu.VMEM((8, 8, RT), F32),
            pltpu.VMEM((3, 8, RT), F32),
            pltpu.VMEM((4, 3, 8, RT), F32),
            pltpu.VMEM((8, 8, RT), F32),
            pltpu.VMEM((8, RT), F32),
            pltpu.VMEM((8, HEAD, RT), F32),
            pltpu.VMEM((RT, WIDE), F32),
            pltpu.VMEM((8, 128, WIDE), F32),
            pltpu.VMEM((8, 128, WIDE), BF16),
            pltpu.VMEM((8, 128, WIDE), BF16),
            pltpu.VMEM((7, 128, WIDE), BF16),
            pltpu.VMEM((7, 128, WIDE), BF16),
            pltpu.VMEM((4, 4, TOK, WIDE), BF16),
            pltpu.VMEM((4, 4, TOK, WIDE), BF16),
            pltpu.VMEM((2, TOK, WIDE), BF16),
            pltpu.VMEM((2, TOK, WIDE), BF16),
            dma((2,)), dma((N_SEM,)), dma((N_SEM,)), dma((2,)), dma((2,)),
        ],
        compiler_params=pltpu.CompilerParams(
            collective_id=0, has_side_effects=True, vmem_limit_bytes=50 * 2**20
        ),
    )(
        stripe_map,
        query_matrix.transpose(1, 0, 2),
        output_gradient.transpose(1, 0, 2),
        key_matrix,
        value_matrix,
    )
    return dq.transpose(1, 0, 2), dkv[:, :HEAD], dkv[:, HEAD:]


def solution(mesh):
    return jax.shard_map(
        per_device,
        mesh=mesh,
        in_specs=(
            P(("blk", "uly"), None, "tp"),
            P(("blk", "uly"), None),
            P(("blk", "uly"), None),
            P(("blk", "uly"), None, "tp"),
            P(),
        ),
        out_specs=(P(("blk", "uly"), None, "tp"), P(("blk", "uly"), "tp"), P(("blk", "uly"), "tp")),
        check_vma=False,
    )
```

```python
import jax
import jax.numpy as jnp
from jax import lax
from jax.experimental import pallas as pl
from jax.experimental.pallas import tpu as pltpu
from jax.sharding import PartitionSpec as P

HEAD = 96
WIDE = 2 * HEAD
TOK = 64
RT = 256
LOG2E = 1.4426950408889634
SCALE = HEAD**-0.5
SCALE2 = SCALE * LOG2E
HIDE = -1e30
FLOOR = -1e29
F32 = jnp.float32
BF16 = jnp.bfloat16
MESH = pl.DeviceIdType.MESH
NT = (((1,), (1,)), ((), ()))
N_SEM = 96


def dot(a, b):
    return jnp.dot(a, b, preferred_element_type=F32)


def kernel(
    stripe, q_in, g_in, k_in, v_in, dq_out, dkv_out,
    qg, kv, qga, kva, kvu, kt, wq, wg, prob, grad,
    tile_top, tile_sum, tile_mix, stat, stat_in, fac, delta,
    dqt, dkf, own, sbs, sbr, l1s, relay, fin, dqb, dqr, l2s, l2r,
    loc_sem, send_sem, recv_sem, l2_s, l2_r,
):
    b, y, t = lax.axis_index("blk"), lax.axis_index("uly"), lax.axis_index("tp")
    x, zl = b // 8, b % 8
    h, c = t // 2, t % 2
    z = h * 8 + zl

    def dev(x_, y_, z_, c_):
        return (x_ * 8 + z_ % 8, y_, (z_ // 8) * 2 + c_)

    def on_x(i):
        return dev((x + i) % 4, y, z, c)

    def on_y(j):
        return dev(x, (y + j) % 4, z, c)

    def on_z(d):
        return dev(x, y, (z + d) % 16, c)

    sib = dev(x, y, z, 1 - c)
    zsteps = (0, 1, 15, 2, 14, 3, 13, jnp.where(c == 0, 4, 12))
    sent = []
    names = {}

    def send(name, src, dst, to):
        n = names.setdefault(name, len(names))
        copy = pltpu.make_async_remote_copy(
            src_ref=src, dst_ref=dst, send_sem=send_sem.at[n], recv_sem=recv_sem.at[n],
            device_id=to, device_id_type=MESH,
        )
        copy.start()
        sent.append(copy)

    def got(name, ref):
        pltpu.make_async_copy(ref, ref, recv_sem.at[names[name]]).wait()

    barrier = pltpu.get_barrier_semaphore()
    peers = [dev((x + i) % 4, (y + j) % 4, z, c) for i in range(4) for j in range(4) if i or j]
    peers += [on_z(d) for d in (1, 15, 2, 14)]
    peers += [dev(x, (y + j) % 4, (z + d) % 16, c) for d in (3, 13, 4, 12) for j in range(4)]
    peers += [sib]

    def greet(to):
        pl.semaphore_signal(barrier, inc=1, device_id=to, device_id_type=MESH)

    for to in peers:
        greet(to)
    mine = (c == 0) & (y % 2 == 0) & (h == y // 2)
    for hs in range(2):

        @pl.when(jnp.logical_not(mine & (h == hs)))
        def _():
            greet(dev(x, t, hs * 8 + zl, ((t - y + 4) % 4) // 2))

    for g in range(4):
        part = slice(g * HEAD, (g + 1) * HEAD)
        kv[g] = jnp.concatenate(
            [k_in[:32, part], v_in[:32, part], k_in[32:, part], v_in[32:, part]], axis=1
        )
        qs, gs = q_in[g], g_in[g]
        qg[g] = jnp.concatenate(
            [qs[:, :HEAD], gs[:, :HEAD], qs[:, HEAD:], gs[:, HEAD:]], axis=1
        )
    pl.semaphore_wait(barrier, len(peers) + 2 - jnp.where(mine, 1, 0))

    half = pl.ds(pl.multiple_of(16 * c, 16), 16)

    def send_kv(n, j):
        send(
            f"k{n}_{j}", kv.at[(y + j) % 4, half], kva.at[c, zl, j],
            dev(x, (y + j) % 4, (z + zsteps[n]) % 16, c),
        )

    loc_kv = pltpu.make_async_copy(kv.at[y, half], kva.at[c, zl, 0], loc_sem.at[0])
    loc_kv.start()
    loc_qg = pltpu.make_async_copy(qg.at[y], qga.at[x, 0], loc_sem.at[1])
    loc_qg.start()
    for j in (1, 3, 2):
        send_kv(0, j)
    for j in (1, 3, 2):
        send(f"qy{j}", qg.at[(y + j) % 4], qga.at[x, j], on_y(j))
    for i in (1, 3):
        send(f"x{i}_0", qg.at[y], qga.at[x, 0], on_x(i))
    for n in (7, 5, 6):
        for j in (0, 1, 3, 2):
            send_kv(n, j)
    for n in range(1, 5):
        send_kv(n, 0)
    for j in (0, 1, 3, 2):
        send(
            f"x2_{j}", qg.at[(y + j) % 4], qga.at[x, j],
            dev((x + 2) % 4, (y + j) % 4, z, c),
        )
    rest = pl.ds(1, 3)

    def share_kv(n):
        zs = (zl + 16 - zsteps[n]) % 8
        if 0 < n < 5:
            got(f"k{n}_0", kva.at[c, zs, 0])
            got(f"k{n}_r", kva.at[c, zs, rest])
        else:
            for j in range(4):
                if n or j:
                    got(f"k{n}_{j}", kva.at[c, zs, j])
        if n == 0:
            for d in range(1, 5):
                send(f"k{d}_r", kva.at[c, zl, rest], kva.at[c, zl, rest], on_z(zsteps[d]))
        send(f"s{n}", kva.at[c, zs], kva.at[c, zs], sib)

    loc_kv.wait()
    share_kv(0)
    for j in (1, 3, 2):
        got(f"qy{j}", qga.at[x, j])
        for i in (1, 3):
            send(f"x{i}_{j}", qga.at[x, j], qga.at[x, j], on_x(i))

    lane = lax.broadcasted_iota(jnp.int32, (1, RT), 1)
    sub = lax.broadcasted_iota(jnp.int32, (TOK, RT), 0)
    low_lanes = lax.broadcasted_iota(jnp.int32, (RT, WIDE), 1) < HEAD

    def order(n):
        return (zl + jnp.where(n % 2 == 1, 8 - (n + 1) // 2, n // 2)) % 8

    def unpack(n):
        zs = order(n)
        for hf in range(2):
            for j in range(4):
                v = kva[hf, zs, j]
                kvu[zs, TOK * j + 16 * hf : TOK * j + 16 * hf + 16, :] = v[:, :WIDE]
                kvu[zs, TOK * j + 32 + 16 * hf : TOK * j + 48 + 16 * hf, :] = v[:, WIDE:]

    def rows_in(xs):
        both = qga[xs].reshape(RT, 2 * WIDE)
        zero = jnp.zeros((RT, WIDE), BF16)
        for m in range(2):
            part = both[:, m * WIDE : (m + 1) * WIDE]
            wq[xs * 2 + m] = jnp.where(low_lanes, part, zero)
            wg[xs * 2 + m] = jnp.where(low_lanes, zero, part)

    def block_of(xs, zs, j):
        return stripe[(xs * 8 + zs) * 4 + (y - j + 4) % 4]

    def rows_of(xs):
        out = jnp.zeros((1, RT), jnp.int32)
        for j in range(4):
            out = jnp.where(lane // TOK == j, block_of(xs, zl, j), out)
        return out

    def tile(xs, row_block, kc, diagonal=False):
        for m in range(2):
            rt = xs * 2 + m
            s = lax.dot_general(kvu[kc], wq[rt], NT, preferred_element_type=F32) * SCALE2
            pg = lax.dot_general(kvu[kc], wg[rt], NT, preferred_element_type=F32)
            pieces, biases = [], []
            top = jnp.full((8, RT), FLOOR, F32)
            for j in range(4):
                piece = s[TOK * j : TOK * (j + 1)]
                key_block = block_of(x, kc, j)
                if diagonal:
                    seen = sub + key_block * TOK <= row_block * TOK + lane % TOK
                    piece = jnp.where(seen, piece, HIDE)
                    bias = jnp.zeros((1, RT), F32)
                else:
                    bias = jnp.where(key_block > row_block, HIDE, 0.0)
                top = jnp.maximum(top, jnp.max(piece.reshape(8, 8, RT), axis=0) + bias)
                pieces.append(piece)
                biases.append(bias)
            top = jnp.max(top, axis=0, keepdims=True)
            total = jnp.zeros((8, RT), F32)
            mixed = jnp.zeros((8, RT), F32)
            for j in range(4):
                e = jnp.exp2(pieces[j] - (top - biases[j]))
                prob[rt, kc, TOK * j : TOK * (j + 1)] = e
                total = total + jnp.sum(e.reshape(8, 8, RT), axis=0)
                mixed = mixed + jnp.sum(
                    (e * pg[TOK * j : TOK * (j + 1)]).reshape(8, 8, RT), axis=0
                )
            grad[rt, kc] = pg
            tile_top[kc, pl.ds(rt, 1)] = top
            tile_sum[kc, pl.ds(rt, 1)] = jnp.sum(total, axis=0, keepdims=True)
            tile_mix[kc, pl.ds(rt, 1)] = jnp.sum(mixed, axis=0, keepdims=True)

    def tiles(xs, lo, count, turns=1):
        row_block = rows_of(xs)

        def step(turn, _):
            for n in range(count):
                tile(xs, row_block, order(lo + turn * count + n))
            return 0

        lax.fori_loop(0, turns, step, 0)

    loc_qg.wait()
    rows_in(x)
    got("s0", kva.at[1 - c, zl])
    unpack(0)
    tile(x, rows_of(x), zl, True)
    for lo, count in ((1, 4), (5, 3)):
        for n in range(lo, lo + count):
            share_kv(n)
        for n in range(lo, lo + count):
            got(f"s{n}", kva.at[1 - c, order(n)])
            unpack(n)
        tiles(x, lo, count)
    for i in (1, 3, 2):
        xs = (x - i + 4) % 4
        for j in range(4):
            got(f"x{i}_{j}", qga.at[xs, j])
        rows_in(xs)
        tiles(xs, 0, 4, 2)

    top = tile_top[0]
    for kc in range(1, 8):
        top = jnp.maximum(top, tile_top[kc])
    total = jnp.zeros((8, RT), F32)
    mixed = jnp.zeros((8, RT), F32)
    for kc in range(8):
        up = jnp.exp2(tile_top[kc] - top)
        total = total + tile_sum[kc] * up
        mixed = mixed + tile_mix[kc] * up
    stat[0] = top
    stat[1] = total
    stat[2] = mixed
    for i in (2, 1, 3):
        send(f"st{i}", stat, stat_in.at[i], on_x(i))
    dqt[...] = jnp.zeros_like(dqt)

    def turn_keys(kc, _):
        kt[kc] = jnp.transpose(kvu[kc].astype(F32))[:HEAD].astype(BF16)
        return 0

    lax.fori_loop(0, 8, turn_keys, 0)
    for i in (1, 3, 2):
        got(f"st{i}", stat_in.at[i])
    all_top = top
    for i in range(1, 4):
        all_top = jnp.maximum(all_top, stat_in[i, 0])
    up = jnp.exp2(top - all_top)
    total = total * up
    mixed = mixed * up
    for i in range(1, 4):
        up = jnp.exp2(stat_in[i, 0] - all_top)
        total = total + stat_in[i, 1] * up
        mixed = mixed + stat_in[i, 2] * up
    inverse = 1.0 / total
    delta[...] = mixed * inverse
    for kc in range(8):
        fac[kc] = jnp.exp2(tile_top[kc] - all_top) * inverse

    steps = (zsteps[7], 3, 13, 2, 14, 1, 15, 0)

    def give(k):
        got(f"sb{k}", sbr.at[k])
        total = own[k] + sbr[k].astype(F32)
        if k in (3, 4):
            got(f"r{k - 2}", relay.at[k - 2])
            if k == 3:
                got("r0", relay.at[0])
            far = relay[0].astype(F32)
            total = total + relay[k - 2].astype(F32)
            total = total + jnp.where(c == k - 3, far, jnp.zeros_like(far))
        l1s[k] = total.astype(BF16)
        if k < 3:
            send(f"r{k}", l1s.at[k], relay.at[k], on_z((jnp.where(c == 0, 2, 14), 1, 15)[k]))
        else:
            send(f"f{k}", l1s.at[k], fin.at[k - 3], on_z(steps[k]))

    def packed(rows):
        return jnp.concatenate([rows[:TOK], rows[TOK:]], axis=1)

    for k in range(8):
        kc = (zl + steps[k]) % 8

        def rows_step(rt, dkv):
            p = prob[rt, kc] * fac[kc, pl.ds(rt, 1)]
            ds = (p * (grad[rt, kc] - delta[pl.ds(rt, 1)])).astype(BF16)
            dkv = dkv + dot(p.astype(BF16), wg[rt]) + dot(ds, wq[rt])
            dqt[rt] += dot(kt[kc], ds)
            return dkv

        dkf[...] = lax.fori_loop(0, 8, rows_step, jnp.zeros((RT, WIDE), F32), unroll=8)
        sbs[k] = packed(dkf[pl.ds(pl.multiple_of(128 * (1 - c), 128), 128)]).astype(BF16)
        own[k] = packed(dkf[pl.ds(pl.multiple_of(128 * c, 128), 128)])
        send(f"sb{k}", sbs.at[k], sbr.at[k], sib)
        if k in (2, 3, 4, 7):
            give(k - 2)

    for i in (2, 1, 3, 0):
        xs = (x + i) % 4
        pair = dqt[pl.ds(xs * 2, 2)].reshape(WIDE, RT)
        rows = (jnp.transpose(pair) * SCALE).reshape(4, TOK, WIDE)
        dqb[i] = jnp.concatenate([rows[:, :32], rows[:, 32:]], axis=2).astype(BF16)
        for j in (2, 1, 3, 0):
            if i or j:
                send(
                    f"dq{i}_{j}", dqb.at[i, j], dqr.at[i, y],
                    dev(xs, (y - j + 4) % 4, z, c),
                )
        if i == 2:
            give(6)
        if i == 1:
            give(3)
            give(4)
    dqr[0, y] = dqb[0, 0]

    got("sb7", sbr.at[7])
    total = own[7] + sbr[7].astype(F32)
    for k in range(3, 7):
        got(f"f{k}", fin.at[k - 3])
        total = total + fin[k - 3].astype(F32)
    left = lax.broadcasted_iota(jnp.int32, (TOK, WIDE), 1) < HEAD
    for q in range(2):
        l2s[q] = (total[:, q * WIDE : (q + 1) * WIDE] * jnp.where(left, SCALE, 1.0)).astype(BF16)
    for q in range(2):
        j = 2 * c + q
        yo = (y - j + 4) % 4
        is_self = mine & (yo == y)
        copy = pltpu.make_async_remote_copy(
            src_ref=l2s.at[q], dst_ref=l2r.at[h], send_sem=l2_s.at[q], recv_sem=l2_r.at[h],
            device_id=dev(x, yo, 8 * (y // 2) + zl, y % 2), device_id_type=MESH,
        )

        @pl.when(jnp.logical_not(is_self))
        def _():
            copy.start()

        @pl.when(is_self)
        def _():
            l2r[h] = l2s[q]

    for j in range(4):
        gs = (y + j) % 4
        total = jnp.zeros((32, 2 * WIDE), F32)
        for i in (0, 1, 3, 2):
            if i or j:
                got(f"dq{i}_{j}", dqr.at[i, gs])
            total = total + dqr[i, gs].astype(F32)
        dq_out[gs, :32] = total[:, :WIDE].astype(BF16)
        dq_out[gs, 32:] = total[:, WIDE:].astype(BF16)

    for hs in range(2):

        @pl.when(jnp.logical_not(mine & (h == hs)))
        def _():
            pltpu.make_async_copy(l2r.at[hs], l2r.at[hs], l2_r.at[hs]).wait()

    dkv_out[...] = (l2r[0].astype(F32) + l2r[1].astype(F32)).astype(BF16)
    for copy in sent:
        copy.wait_send()
    for q in range(2):
        yo = (y - 2 * c - q + 4) % 4

        @pl.when(jnp.logical_not(mine & (yo == y)))
        def _():
            pltpu.make_async_copy(l2s.at[q], l2s.at[q], l2_s.at[q]).wait()


def per_device(query_matrix, key_matrix, value_matrix, output_gradient, stripe_map):
    vmem = pl.BlockSpec(memory_space=pltpu.VMEM)
    dma = pltpu.SemaphoreType.DMA
    dq, dkv = pl.pallas_call(
        kernel,
        out_shape=[
            jax.ShapeDtypeStruct((4, TOK, WIDE), BF16),
            jax.ShapeDtypeStruct((TOK, WIDE), BF16),
        ],
        in_specs=[pl.BlockSpec(memory_space=pltpu.SMEM)] + [vmem] * 4,
        out_specs=[vmem, vmem],
        scratch_shapes=[
            pltpu.VMEM((4, TOK, 2 * WIDE), BF16),
            pltpu.VMEM((4, 32, 2 * WIDE), BF16),
            pltpu.VMEM((4, 4, TOK, 2 * WIDE), BF16),
            pltpu.VMEM((2, 8, 4, 16, 2 * WIDE), BF16),
            pltpu.VMEM((8, RT, WIDE), BF16),
            pltpu.VMEM((8, HEAD, RT), BF16),
            pltpu.VMEM((8, RT, WIDE), BF16),
            pltpu.VMEM((8, RT, WIDE), BF16),
            pltpu.VMEM((8, 8, RT, RT), F32),
            pltpu.VMEM((8, 8, RT, RT), F32),
            pltpu.VMEM((8, 8, RT), F32),
            pltpu.VMEM((8, 8, RT), F32),
            pltpu.VMEM((8, 8, RT), F32),
            pltpu.VMEM((3, 8, RT), F32),
            pltpu.VMEM((4, 3, 8, RT), F32),
            pltpu.VMEM((8, 8, RT), F32),
            pltpu.VMEM((8, RT), F32),
            pltpu.VMEM((8, HEAD, RT), F32),
            pltpu.VMEM((RT, WIDE), F32),
            pltpu.VMEM((8, TOK, 2 * WIDE), F32),
            pltpu.VMEM((8, TOK, 2 * WIDE), BF16),
            pltpu.VMEM((8, TOK, 2 * WIDE), BF16),
            pltpu.VMEM((7, TOK, 2 * WIDE), BF16),
            pltpu.VMEM((3, TOK, 2 * WIDE), BF16),
            pltpu.VMEM((4, TOK, 2 * WIDE), BF16),
            pltpu.VMEM((4, 4, 32, 2 * WIDE), BF16),
            pltpu.VMEM((4, 4, 32, 2 * WIDE), BF16),
            pltpu.VMEM((2, TOK, WIDE), BF16),
            pltpu.VMEM((2, TOK, WIDE), BF16),
            dma((2,)), dma((N_SEM,)), dma((N_SEM,)), dma((2,)), dma((2,)),
        ],
        compiler_params=pltpu.CompilerParams(
            collective_id=0, has_side_effects=True, vmem_limit_bytes=50 * 2**20
        ),
    )(
        stripe_map,
        query_matrix.transpose(1, 0, 2),
        output_gradient.transpose(1, 0, 2),
        key_matrix,
        value_matrix,
    )
    return dq.transpose(1, 0, 2), dkv[:, :HEAD], dkv[:, HEAD:]


def solution(mesh):
    return jax.shard_map(
        per_device,
        mesh=mesh,
        in_specs=(
            P(("blk", "uly"), None, "tp"),
            P(("blk", "uly"), None),
            P(("blk", "uly"), None),
            P(("blk", "uly"), None, "tp"),
            P(),
        ),
        out_specs=(P(("blk", "uly"), None, "tp"), P(("blk", "uly"), "tp"), P(("blk", "uly"), "tp")),
        check_vma=False,
    )
```

```python
import jax
import jax.numpy as jnp
from jax import lax
from jax.experimental import pallas as pl
from jax.experimental.pallas import tpu as pltpu
from jax.sharding import PartitionSpec as P

HEAD = 96
WIDE = 2 * HEAD
TOK = 64
RT = 256
LOG2E = 1.4426950408889634
SCALE = HEAD**-0.5
SCALE2 = SCALE * LOG2E
HIDE = -1e30
FLOOR = -1e29
F32 = jnp.float32
BF16 = jnp.bfloat16
MESH = pl.DeviceIdType.MESH
NT = (((1,), (1,)), ((), ()))
N_SEM = 96


def dot(a, b):
    return jnp.dot(a, b, preferred_element_type=F32)


def kernel(
    stripe, q_in, g_in, k_in, v_in, dq_out, dkv_out,
    qg, kv, qga, kva, kvu, kt, wq, wg, prob, grad,
    tile_top, tile_sum, tile_mix, stat, stat_in, fac, delta,
    dqt, dkf, own, sbs, sbr, l1s, relay, fin, fwd, dks, dqb, dqr,
    loc_sem, send_sem, recv_sem, f_s, f_r, r_s, r_r, w_r,
):
    b, y, t = lax.axis_index("blk"), lax.axis_index("uly"), lax.axis_index("tp")
    x, zl = b // 8, b % 8
    h, c = t // 2, t % 2
    z = h * 8 + zl

    def dev(x_, y_, z_, c_):
        return (x_ * 8 + z_ % 8, y_, (z_ // 8) * 2 + c_)

    def on_x(i):
        return dev((x + i) % 4, y, z, c)

    def on_y(j):
        return dev(x, (y + j) % 4, z, c)

    def on_z(d):
        return dev(x, y, (z + d) % 16, c)

    sib = dev(x, y, z, 1 - c)
    zsteps = (0, 1, 15, 2, 14, 3, 13, jnp.where(c == 0, 4, 12))
    sent = []
    names = {}

    def send(name, src, dst, to):
        n = names.setdefault(name, len(names))
        copy = pltpu.make_async_remote_copy(
            src_ref=src, dst_ref=dst, send_sem=send_sem.at[n], recv_sem=recv_sem.at[n],
            device_id=to, device_id_type=MESH,
        )
        copy.start()
        sent.append(copy)

    def got(name, ref):
        pltpu.make_async_copy(ref, ref, recv_sem.at[names[name]]).wait()

    barrier = pltpu.get_barrier_semaphore()
    peers = [dev((x + i) % 4, (y + j) % 4, z, c) for i in range(4) for j in range(4) if i or j]
    peers += [on_z(d) for d in (1, 15, 2, 14)]
    peers += [dev(x, (y + j) % 4, (z + d) % 16, c) for d in (3, 13, 4, 12) for j in range(4)]
    peers += [sib]

    def greet(to):
        pl.semaphore_signal(barrier, inc=1, device_id=to, device_id_type=MESH)

    for to in peers:
        greet(to)
    home = y // 2
    mine = (c == 0) & (y % 2 == 0) & (h == home)
    near = (0, 1, 15, 2, 14, 3, 13)
    straight = [((z + d) % 16) // 8 == home for d in near]
    n_targets = 2
    for flag in straight:
        n_targets = n_targets + jnp.where(flag, 2, 0)
    giver = ((t - y + 4) % 4) // 2
    for d in near + (4, 12):
        to = dev(x, t, (z + d) % 16, giver)
        if d:
            greet(to)
        else:

            @pl.when(jnp.logical_not(mine))
            def _():
                greet(to)

    for g in range(4):
        part = slice(g * HEAD, (g + 1) * HEAD)
        kv[g] = jnp.concatenate(
            [k_in[:32, part], v_in[:32, part], k_in[32:, part], v_in[32:, part]], axis=1
        )
        qs, gs = q_in[g], g_in[g]
        qg[g] = jnp.concatenate(
            [qs[:, :HEAD], gs[:, :HEAD], qs[:, HEAD:], gs[:, HEAD:]], axis=1
        )
    pl.semaphore_wait(barrier, len(peers) + n_targets - jnp.where(mine, 1, 0))

    half = pl.ds(pl.multiple_of(16 * c, 16), 16)

    def send_kv(n, j):
        send(
            f"k{n}_{j}", kv.at[(y + j) % 4, half], kva.at[c, zl, j],
            dev(x, (y + j) % 4, (z + zsteps[n]) % 16, c),
        )

    loc_kv = pltpu.make_async_copy(kv.at[y, half], kva.at[c, zl, 0], loc_sem.at[0])
    loc_kv.start()
    loc_qg = pltpu.make_async_copy(qg.at[y], qga.at[x, 0], loc_sem.at[1])
    loc_qg.start()
    for j in (1, 3, 2):
        send_kv(0, j)
    for j in (1, 3, 2):
        send(f"qy{j}", qg.at[(y + j) % 4], qga.at[x, j], on_y(j))
    for i in (1, 3):
        send(f"x{i}_0", qg.at[y], qga.at[x, 0], on_x(i))
    for n in (7, 5, 6):
        for j in (0, 1, 3, 2):
            send_kv(n, j)
    for n in range(1, 5):
        send_kv(n, 0)
    for j in (0, 1, 3, 2):
        send(
            f"x2_{j}", qg.at[(y + j) % 4], qga.at[x, j],
            dev((x + 2) % 4, (y + j) % 4, z, c),
        )
    rest = pl.ds(1, 3)

    def share_kv(n):
        zs = (zl + 16 - zsteps[n]) % 8
        if 0 < n < 5:
            got(f"k{n}_0", kva.at[c, zs, 0])
            got(f"k{n}_r", kva.at[c, zs, rest])
        else:
            for j in range(4):
                if n or j:
                    got(f"k{n}_{j}", kva.at[c, zs, j])
        if n == 0:
            for d in range(1, 5):
                send(f"k{d}_r", kva.at[c, zl, rest], kva.at[c, zl, rest], on_z(zsteps[d]))
        send(f"s{n}", kva.at[c, zs], kva.at[c, zs], sib)

    loc_kv.wait()
    share_kv(0)
    for j in (1, 3, 2):
        got(f"qy{j}", qga.at[x, j])
        for i in (1, 3):
            send(f"x{i}_{j}", qga.at[x, j], qga.at[x, j], on_x(i))

    lane = lax.broadcasted_iota(jnp.int32, (1, RT), 1)
    sub = lax.broadcasted_iota(jnp.int32, (TOK, RT), 0)
    low_lanes = lax.broadcasted_iota(jnp.int32, (RT, WIDE), 1) < HEAD

    def order(n):
        return (zl + jnp.where(n % 2 == 1, 8 - (n + 1) // 2, n // 2)) % 8

    def unpack(n):
        zs = order(n)
        for hf in range(2):
            for j in range(4):
                v = kva[hf, zs, j]
                kvu[zs, TOK * j + 16 * hf : TOK * j + 16 * hf + 16, :] = v[:, :WIDE]
                kvu[zs, TOK * j + 32 + 16 * hf : TOK * j + 48 + 16 * hf, :] = v[:, WIDE:]

    def rows_in(xs):
        both = qga[xs].reshape(RT, 2 * WIDE)
        zero = jnp.zeros((RT, WIDE), BF16)
        for m in range(2):
            part = both[:, m * WIDE : (m + 1) * WIDE]
            wq[xs * 2 + m] = jnp.where(low_lanes, part, zero)
            wg[xs * 2 + m] = jnp.where(low_lanes, zero, part)

    def block_of(xs, zs, j):
        return stripe[(xs * 8 + zs) * 4 + (y - j + 4) % 4]

    def rows_of(xs):
        out = jnp.zeros((1, RT), jnp.int32)
        for j in range(4):
            out = jnp.where(lane // TOK == j, block_of(xs, zl, j), out)
        return out

    def tile(xs, row_block, kc, diagonal=False):
        for m in range(2):
            rt = xs * 2 + m
            s = lax.dot_general(kvu[kc], wq[rt], NT, preferred_element_type=F32) * SCALE2
            pg = lax.dot_general(kvu[kc], wg[rt], NT, preferred_element_type=F32)
            pieces, biases = [], []
            top = jnp.full((8, RT), FLOOR, F32)
            for j in range(4):
                piece = s[TOK * j : TOK * (j + 1)]
                key_block = block_of(x, kc, j)
                if diagonal:
                    seen = sub + key_block * TOK <= row_block * TOK + lane % TOK
                    piece = jnp.where(seen, piece, HIDE)
                    bias = jnp.zeros((1, RT), F32)
                else:
                    bias = jnp.where(key_block > row_block, HIDE, 0.0)
                top = jnp.maximum(top, jnp.max(piece.reshape(8, 8, RT), axis=0) + bias)
                pieces.append(piece)
                biases.append(bias)
            top = jnp.max(top, axis=0, keepdims=True)
            total = jnp.zeros((8, RT), F32)
            mixed = jnp.zeros((8, RT), F32)
            for j in range(4):
                e = jnp.exp2(pieces[j] - (top - biases[j]))
                prob[rt, kc, TOK * j : TOK * (j + 1)] = e
                total = total + jnp.sum(e.reshape(8, 8, RT), axis=0)
                mixed = mixed + jnp.sum(
                    (e * pg[TOK * j : TOK * (j + 1)]).reshape(8, 8, RT), axis=0
                )
            grad[rt, kc] = pg
            tile_top[kc, pl.ds(rt, 1)] = top
            tile_sum[kc, pl.ds(rt, 1)] = jnp.sum(total, axis=0, keepdims=True)
            tile_mix[kc, pl.ds(rt, 1)] = jnp.sum(mixed, axis=0, keepdims=True)

    def tiles(xs, lo, count, turns=1):
        row_block = rows_of(xs)

        def step(turn, _):
            for n in range(count):
                tile(xs, row_block, order(lo + turn * count + n))
            return 0

        lax.fori_loop(0, turns, step, 0)

    loc_qg.wait()
    rows_in(x)
    got("s0", kva.at[1 - c, zl])
    unpack(0)
    tile(x, rows_of(x), zl, True)

    def take_keys(lo, count):
        for n in range(lo, lo + count):
            share_kv(n)
        for n in range(lo, lo + count):
            got(f"s{n}", kva.at[1 - c, order(n)])
            unpack(n)

    def take_rows(i):
        xs = (x - i + 4) % 4
        for j in range(4):
            got(f"x{i}_{j}", qga.at[xs, j])
        rows_in(xs)
        return xs

    take_keys(1, 4)
    tiles(x, 1, 4)
    across = take_rows(2)
    tiles(across, 0, 4)
    take_keys(5, 3)
    tiles(x, 5, 3)
    tiles(across, 4, 4)
    for i in (1, 3):
        tiles(take_rows(i), 0, 4, 2)

    top = tile_top[0]
    for kc in range(1, 8):
        top = jnp.maximum(top, tile_top[kc])
    total = jnp.zeros((8, RT), F32)
    mixed = jnp.zeros((8, RT), F32)
    for kc in range(8):
        up = jnp.exp2(tile_top[kc] - top)
        total = total + tile_sum[kc] * up
        mixed = mixed + tile_mix[kc] * up
    stat[0] = top
    stat[1] = total
    stat[2] = mixed
    for i in (2, 1, 3):
        send(f"st{i}", stat, stat_in.at[i], on_x(i))
    dqt[...] = jnp.zeros_like(dqt)

    def turn_keys(kc, _):
        kt[kc] = jnp.transpose(kvu[kc].astype(F32))[:HEAD].astype(BF16)
        return 0

    lax.fori_loop(0, 8, turn_keys, 0)
    for i in (1, 3, 2):
        got(f"st{i}", stat_in.at[i])
    all_top = top
    for i in range(1, 4):
        all_top = jnp.maximum(all_top, stat_in[i, 0])
    up = jnp.exp2(top - all_top)
    total = total * up
    mixed = mixed * up
    for i in range(1, 4):
        up = jnp.exp2(stat_in[i, 0] - all_top)
        total = total + stat_in[i, 1] * up
        mixed = mixed + stat_in[i, 2] * up
    inverse = 1.0 / total
    delta[...] = mixed * inverse
    for kc in range(8):
        fac[kc] = jnp.exp2(tile_top[kc] - all_top) * inverse

    steps = near + (4,)
    relays = (jnp.where(c == 0, 12, 4), 13, 3, 14, 2, 15, 1)
    slots = (3, 2, 2, 1, 1, 0, 0)
    guarded = []

    def send_if(flag, src, dst, ss, rs, to):
        copy = pltpu.make_async_remote_copy(
            src_ref=src, dst_ref=dst, send_sem=ss, recv_sem=rs, device_id=to, device_id_type=MESH
        )

        @pl.when(flag)
        def _():
            copy.start()

        guarded.append((flag, copy))

    def owner(q, d):
        return dev(x, (y - 2 * c - q + 4) % 4, (z + d) % 16, y % 2)

    def give(k):
        got(f"sb{k}", sbr.at[k])
        l1s[k] = (own[k] + sbr[k].astype(F32)).astype(BF16)
        for q in range(2):
            flag = straight[k]
            if k == 0 and q == 0:
                flag = flag & jnp.logical_not(mine)
            send_if(flag, l1s.at[k, q], fin.at[k], f_s.at[k, q], f_r.at[k], owner(q, near[k]))
        send_if(
            jnp.logical_not(straight[k]), l1s.at[k], relay.at[slots[k]],
            r_s.at[k], r_r.at[slots[k]], on_z(relays[k]),
        )

    def packed(rows):
        rows = rows.reshape(2, TOK, WIDE)
        return jnp.concatenate([rows[:, :32], rows[:, 32:]], axis=2)

    for k in range(8):
        kc = (zl + steps[k]) % 8

        def rows_step(rt, dkv):
            p = prob[rt, kc] * fac[kc, pl.ds(rt, 1)]
            ds = (p * (grad[rt, kc] - delta[pl.ds(rt, 1)])).astype(BF16)
            dkv = dkv + dot(p.astype(BF16), wg[rt]) + dot(ds, wq[rt])
            dqt[rt] += dot(kt[kc], ds)
            return dkv

        dkf[...] = lax.fori_loop(0, 8, rows_step, jnp.zeros((RT, WIDE), F32), unroll=8)
        sbs[k] = packed(dkf[pl.ds(pl.multiple_of(128 * (1 - c), 128), 128)]).astype(BF16)
        own[k] = packed(dkf[pl.ds(pl.multiple_of(128 * c, 128), 128)])
        send(f"sb{k}", sbs.at[k], sbr.at[k], sib)
        if k >= 2:
            give(k - 2)

    give(6)
    for i in (2, 1, 3, 0):
        xs = (x + i) % 4
        pair = dqt[pl.ds(xs * 2, 2)].reshape(WIDE, RT)
        rows = (jnp.transpose(pair) * SCALE).reshape(4, TOK, WIDE)
        dqb[i] = jnp.concatenate([rows[:, :32], rows[:, 32:]], axis=2).astype(BF16)
        for j in (2, 1, 3, 0):
            if i or j:
                send(
                    f"dq{i}_{j}", dqb.at[i, j], dqr.at[i, y],
                    dev(xs, (y - j + 4) % 4, z, c),
                )
    dqr[0, y] = dqb[0, 0]

    got("sb7", sbr.at[7])
    total = own[7] + sbr[7].astype(F32)
    for k in range(3):
        pltpu.make_async_copy(relay.at[k], relay.at[k], r_r.at[k]).wait()
        total = total + relay[k].astype(F32)
    ahead = ((z - 8 * home + 16 + 12) % 16) < 8
    fourth = ahead == (c == 0)
    dks[...] = total

    @pl.when(fourth)
    def _():
        pltpu.make_async_copy(relay.at[3], relay.at[3], r_r.at[3]).wait()
        dks[...] += relay[3].astype(F32)

    l1s[7] = dks[...].astype(BF16)
    side = jnp.where(ahead, 0, 1)
    for q in range(2):
        send_if(
            c >= 0, l1s.at[7, q], fwd.at[side], f_s.at[7, q], w_r.at[side],
            owner(q, jnp.where(ahead, 12, 4)),
        )

    @pl.when(mine)
    def _():
        fin[0] = l1s[0, 0]

    for j in range(4):
        gs = (y + j) % 4
        total = jnp.zeros((32, 2 * WIDE), F32)
        for i in (0, 1, 3, 2):
            if i or j:
                got(f"dq{i}_{j}", dqr.at[i, gs])
            total = total + dqr[i, gs].astype(F32)
        dq_out[gs, :32] = total[:, :WIDE].astype(BF16)
        dq_out[gs, 32:] = total[:, WIDE:].astype(BF16)

    @pl.when(jnp.logical_not(mine))
    def _():
        pltpu.make_async_copy(fin.at[0], fin.at[0], f_r.at[0]).wait()

    total = fin[0].astype(F32)
    for k in range(1, 7):
        pltpu.make_async_copy(fin.at[k], fin.at[k], f_r.at[k]).wait()
        total = total + fin[k].astype(F32)
    for side in range(2):
        pltpu.make_async_copy(fwd.at[side], fwd.at[side], w_r.at[side]).wait()
        total = total + fwd[side].astype(F32)
    left = lax.broadcasted_iota(jnp.int32, (32, WIDE), 1) < HEAD
    scale = jnp.where(left, SCALE, 1.0)
    dkv_out[:32] = (total[:, :WIDE] * scale).astype(BF16)
    dkv_out[32:] = (total[:, WIDE:] * scale).astype(BF16)
    for copy in sent:
        copy.wait_send()
    for flag, copy in guarded:
        pl.when(flag)(copy.wait_send)


def per_device(query_matrix, key_matrix, value_matrix, output_gradient, stripe_map):
    vmem = pl.BlockSpec(memory_space=pltpu.VMEM)
    dma = pltpu.SemaphoreType.DMA
    dq, dkv = pl.pallas_call(
        kernel,
        out_shape=[
            jax.ShapeDtypeStruct((4, TOK, WIDE), BF16),
            jax.ShapeDtypeStruct((TOK, WIDE), BF16),
        ],
        in_specs=[pl.BlockSpec(memory_space=pltpu.SMEM)] + [vmem] * 4,
        out_specs=[vmem, vmem],
        scratch_shapes=[
            pltpu.VMEM((4, TOK, 2 * WIDE), BF16),
            pltpu.VMEM((4, 32, 2 * WIDE), BF16),
            pltpu.VMEM((4, 4, TOK, 2 * WIDE), BF16),
            pltpu.VMEM((2, 8, 4, 16, 2 * WIDE), BF16),
            pltpu.VMEM((8, RT, WIDE), BF16),
            pltpu.VMEM((8, HEAD, RT), BF16),
            pltpu.VMEM((8, RT, WIDE), BF16),
            pltpu.VMEM((8, RT, WIDE), BF16),
            pltpu.VMEM((8, 8, RT, RT), F32),
            pltpu.VMEM((8, 8, RT, RT), F32),
            pltpu.VMEM((8, 8, RT), F32),
            pltpu.VMEM((8, 8, RT), F32),
            pltpu.VMEM((8, 8, RT), F32),
            pltpu.VMEM((3, 8, RT), F32),
            pltpu.VMEM((4, 3, 8, RT), F32),
            pltpu.VMEM((8, 8, RT), F32),
            pltpu.VMEM((8, RT), F32),
            pltpu.VMEM((8, HEAD, RT), F32),
            pltpu.VMEM((RT, WIDE), F32),
            pltpu.VMEM((8, 2, 32, 2 * WIDE), F32),
            pltpu.VMEM((8, 2, 32, 2 * WIDE), BF16),
            pltpu.VMEM((8, 2, 32, 2 * WIDE), BF16),
            pltpu.VMEM((8, 2, 32, 2 * WIDE), BF16),
            pltpu.VMEM((4, 2, 32, 2 * WIDE), BF16),
            pltpu.VMEM((7, 32, 2 * WIDE), BF16),
            pltpu.VMEM((2, 32, 2 * WIDE), BF16),
            pltpu.VMEM((2, 32, 2 * WIDE), F32),
            pltpu.VMEM((4, 4, 32, 2 * WIDE), BF16),
            pltpu.VMEM((4, 4, 32, 2 * WIDE), BF16),
            dma((2,)), dma((N_SEM,)), dma((N_SEM,)),
            dma((8, 2)), dma((7,)), dma((7,)), dma((4,)), dma((2,)),
        ],
        compiler_params=pltpu.CompilerParams(
            collective_id=0, has_side_effects=True, vmem_limit_bytes=50 * 2**20
        ),
    )(
        stripe_map,
        query_matrix.transpose(1, 0, 2),
        output_gradient.transpose(1, 0, 2),
        key_matrix,
        value_matrix,
    )
    return dq.transpose(1, 0, 2), dkv[:, :HEAD], dkv[:, HEAD:]


def solution(mesh):
    return jax.shard_map(
        per_device,
        mesh=mesh,
        in_specs=(
            P(("blk", "uly"), None, "tp"),
            P(("blk", "uly"), None),
            P(("blk", "uly"), None),
            P(("blk", "uly"), None, "tp"),
            P(),
        ),
        out_specs=(P(("blk", "uly"), None, "tp"), P(("blk", "uly"), "tp"), P(("blk", "uly"), "tp")),
        check_vma=False,
    )
```

```python
import jax
import jax.numpy as jnp
from jax import lax
from jax.experimental import pallas as pl
from jax.experimental.pallas import tpu as pltpu
from jax.sharding import PartitionSpec as P

HEAD = 96
WIDE = 2 * HEAD
TOK = 64
RT = 256
LOG2E = 1.4426950408889634
SCALE = HEAD**-0.5
SCALE2 = SCALE * LOG2E
HIDE = -1e30
FLOOR = -1e29
F32 = jnp.float32
BF16 = jnp.bfloat16
MESH = pl.DeviceIdType.MESH
NT = (((1,), (1,)), ((), ()))
N_SEM = 96


def dot(a, b):
    return jnp.dot(a, b, preferred_element_type=F32)


def kernel(
    stripe, q_in, g_in, k_in, v_in, dq_out, dkv_out,
    qg, kv, qga, kva, kvu, kt, wq, wg, prob, grad,
    tile_top, tile_sum, tile_mix, stat, stat_in, fac, delta,
    dqt, dkf, own, sbs, sbr, l1s, relay, fin, fwd, dks, dqb, dqr,
    loc_sem, send_sem, recv_sem, f_s, f_r, r_s, r_r, w_r, sb_s, sb_r, dq_s, dq_r,
):
    b, y, t = lax.axis_index("blk"), lax.axis_index("uly"), lax.axis_index("tp")
    x, zl = b // 8, b % 8
    h, c = t // 2, t % 2
    z = h * 8 + zl

    def dev(x_, y_, z_, c_):
        return (x_ * 8 + z_ % 8, y_, (z_ // 8) * 2 + c_)

    def on_x(i):
        return dev((x + i) % 4, y, z, c)

    def on_y(j):
        return dev(x, (y + j) % 4, z, c)

    def on_z(d):
        return dev(x, y, (z + d) % 16, c)

    sib = dev(x, y, z, 1 - c)
    zsteps = (0, 1, 15, 2, 14, 3, 13, jnp.where(c == 0, 4, 12))
    sent = []
    names = {}

    def send(name, src, dst, to, keep=True):
        n = names.setdefault(name, len(names))
        copy = pltpu.make_async_remote_copy(
            src_ref=src, dst_ref=dst, send_sem=send_sem.at[n], recv_sem=recv_sem.at[n],
            device_id=to, device_id_type=MESH,
        )
        copy.start()
        if keep:
            sent.append(copy)

    def got(name, ref):
        pltpu.make_async_copy(ref, ref, recv_sem.at[names[name]]).wait()

    barrier = pltpu.get_barrier_semaphore()
    peers = [dev((x + i) % 4, (y + j) % 4, z, c) for i in range(4) for j in range(4) if i or j]
    peers += [on_z(d) for d in (1, 15, 2, 14)]
    peers += [dev(x, (y + j) % 4, (z + d) % 16, c) for d in (3, 13, 4, 12) for j in range(4)]
    peers += [sib]

    def greet(to):
        pl.semaphore_signal(barrier, inc=1, device_id=to, device_id_type=MESH)

    for to in peers:
        greet(to)
    home = y // 2
    mine = (c == 0) & (y % 2 == 0) & (h == home)
    near = (0, 1, 15, 2, 14, 3, 13)
    straight = [((z + d) % 16) // 8 == home for d in near]
    n_targets = 2
    for flag in straight:
        n_targets = n_targets + jnp.where(flag, 2, 0)
    giver = ((t - y + 4) % 4) // 2
    for d in near + (4, 12):
        to = dev(x, t, (z + d) % 16, giver)
        if d:
            greet(to)
        else:

            @pl.when(jnp.logical_not(mine))
            def _():
                greet(to)

    for g in range(4):
        part = slice(g * HEAD, (g + 1) * HEAD)
        kv[g] = jnp.concatenate(
            [k_in[:32, part], v_in[:32, part], k_in[32:, part], v_in[32:, part]], axis=1
        )
        qs, gs = q_in[g], g_in[g]
        qg[g] = jnp.concatenate(
            [qs[:, :HEAD], gs[:, :HEAD], qs[:, HEAD:], gs[:, HEAD:]], axis=1
        )
    pl.semaphore_wait(barrier, len(peers) + n_targets - jnp.where(mine, 1, 0))

    half = pl.ds(pl.multiple_of(16 * c, 16), 16)

    def send_kv(n, j):
        send(
            f"k{n}_{j}", kv.at[(y + j) % 4, half], kva.at[c, zl, j],
            dev(x, (y + j) % 4, (z + zsteps[n]) % 16, c),
        )

    loc_kv = pltpu.make_async_copy(kv.at[y, half], kva.at[c, zl, 0], loc_sem.at[0])
    loc_kv.start()
    loc_qg = pltpu.make_async_copy(qg.at[y], qga.at[x, 0], loc_sem.at[1])
    loc_qg.start()
    for j in (1, 3, 2):
        send_kv(0, j)
    for j in (1, 3, 2):
        send(f"qy{j}", qg.at[(y + j) % 4], qga.at[x, j], on_y(j))
    for i in (1, 3):
        send(f"x{i}_0", qg.at[y], qga.at[x, 0], on_x(i))
    for n in (7, 5, 6):
        for j in (0, 1, 3, 2):
            send_kv(n, j)
    for n in range(1, 5):
        send_kv(n, 0)
    for j in (0, 1, 3, 2):
        send(
            f"x2_{j}", qg.at[(y + j) % 4], qga.at[x, j],
            dev((x + 2) % 4, (y + j) % 4, z, c),
        )
    rest = pl.ds(1, 3)

    def share_kv(n):
        zs = (zl + 16 - zsteps[n]) % 8
        if 0 < n < 5:
            got(f"k{n}_0", kva.at[c, zs, 0])
            got(f"k{n}_r", kva.at[c, zs, rest])
        else:
            for j in range(4):
                if n or j:
                    got(f"k{n}_{j}", kva.at[c, zs, j])
        if n == 0:
            for d in range(1, 5):
                send(f"k{d}_r", kva.at[c, zl, rest], kva.at[c, zl, rest], on_z(zsteps[d]))
        send(f"s{n}", kva.at[c, zs], kva.at[c, zs], sib, False)

    loc_kv.wait()
    share_kv(0)
    for j in (1, 3, 2):
        got(f"qy{j}", qga.at[x, j])
        for i in (1, 3):
            send(f"x{i}_{j}", qga.at[x, j], qga.at[x, j], on_x(i))

    lane = lax.broadcasted_iota(jnp.int32, (1, RT), 1)
    sub = lax.broadcasted_iota(jnp.int32, (TOK, RT), 0)
    low_lanes = lax.broadcasted_iota(jnp.int32, (RT, WIDE), 1) < HEAD

    def order(n):
        return (zl + jnp.where(n % 2 == 1, 8 - (n + 1) // 2, n // 2)) % 8

    def unpack(n):
        zs = order(n)
        for hf in range(2):
            for j in range(4):
                v = kva[hf, zs, j]
                kvu[zs, TOK * j + 16 * hf : TOK * j + 16 * hf + 16, :] = v[:, :WIDE]
                kvu[zs, TOK * j + 32 + 16 * hf : TOK * j + 48 + 16 * hf, :] = v[:, WIDE:]

    def rows_in(xs):
        both = qga[xs].reshape(RT, 2 * WIDE)
        zero = jnp.zeros((RT, WIDE), BF16)
        for m in range(2):
            part = both[:, m * WIDE : (m + 1) * WIDE]
            wq[xs * 2 + m] = jnp.where(low_lanes, part, zero)
            wg[xs * 2 + m] = jnp.where(low_lanes, zero, part)

    def block_of(xs, zs, j):
        return stripe[(xs * 8 + zs) * 4 + (y - j + 4) % 4]

    def rows_of(xs):
        out = jnp.zeros((1, RT), jnp.int32)
        for j in range(4):
            out = jnp.where(lane // TOK == j, block_of(xs, zl, j), out)
        return out

    def tile(xs, row_block, kc, diagonal=False):
        for m in range(2):
            rt = xs * 2 + m
            s = lax.dot_general(kvu[kc], wq[rt], NT, preferred_element_type=F32) * SCALE2
            pg = lax.dot_general(kvu[kc], wg[rt], NT, preferred_element_type=F32)
            pieces, biases = [], []
            top = jnp.full((8, RT), FLOOR, F32)
            for j in range(4):
                piece = s[TOK * j : TOK * (j + 1)]
                key_block = block_of(x, kc, j)
                if diagonal:
                    seen = sub + key_block * TOK <= row_block * TOK + lane % TOK
                    piece = jnp.where(seen, piece, HIDE)
                    bias = jnp.zeros((1, RT), F32)
                else:
                    bias = jnp.where(key_block > row_block, HIDE, 0.0)
                top = jnp.maximum(top, jnp.max(piece.reshape(8, 8, RT), axis=0) + bias)
                pieces.append(piece)
                biases.append(bias)
            top = jnp.max(top, axis=0, keepdims=True)
            total = jnp.zeros((8, RT), F32)
            mixed = jnp.zeros((8, RT), F32)
            for j in range(4):
                e = jnp.exp2(pieces[j] - (top - biases[j]))
                prob[rt, kc, TOK * j : TOK * (j + 1)] = e
                total = total + jnp.sum(e.reshape(8, 8, RT), axis=0)
                mixed = mixed + jnp.sum(
                    (e * pg[TOK * j : TOK * (j + 1)]).reshape(8, 8, RT), axis=0
                )
            grad[rt, kc] = pg
            tile_top[kc, pl.ds(rt, 1)] = top
            tile_sum[kc, pl.ds(rt, 1)] = jnp.sum(total, axis=0, keepdims=True)
            tile_mix[kc, pl.ds(rt, 1)] = jnp.sum(mixed, axis=0, keepdims=True)

    loc_qg.wait()
    rows_in(x)
    got("s0", kva.at[1 - c, zl])

    def unpacks(lo, hi):
        def step(n, _):
            unpack(n)
            return 0

        lax.fori_loop(lo, hi, step, 0)

    def take_keys(lo, hi):
        for n in range(lo, hi):
            share_kv(n)
        for n in range(lo, hi):
            got(f"s{n}", kva.at[1 - c, order(n)])

    def take_rows(i):
        xs = (x - i + 4) % 4
        for j in range(4):
            got(f"x{i}_{j}", qga.at[xs, j])
        rows_in(xs)

    take_keys(1, 4)
    unpacks(0, 4)

    def quad(n, _):
        xs = (x + jnp.where(n < 4, 2 * (n % 2), jnp.where(n < 6, 3, 1))) % 4
        lo = 4 * jnp.where(n < 4, n // 2, n % 2)

        @pl.when(n == 1)
        def _():
            tile(x, rows_of(x), zl, True)
            take_rows(2)

        @pl.when(n == 2)
        def _():
            take_keys(4, 8)
            unpacks(4, 8)

        @pl.when(n == 4)
        def _():
            take_rows(1)

        @pl.when(n == 6)
        def _():
            take_rows(3)

        row_block = rows_of(xs)
        for m in range(4):
            tile(xs, row_block, order(lo + m))
        return 0

    lax.fori_loop(0, 8, quad, 0)

    top = tile_top[0]
    for kc in range(1, 8):
        top = jnp.maximum(top, tile_top[kc])
    total = jnp.zeros((8, RT), F32)
    mixed = jnp.zeros((8, RT), F32)
    for kc in range(8):
        up = jnp.exp2(tile_top[kc] - top)
        total = total + tile_sum[kc] * up
        mixed = mixed + tile_mix[kc] * up
    stat[0] = top
    stat[1] = total
    stat[2] = mixed
    for i in (2, 1, 3):
        send(f"st{i}", stat, stat_in.at[i], on_x(i))
    dqt[...] = jnp.zeros_like(dqt)

    def turn_keys(kc, _):
        kt[kc] = jnp.transpose(kvu[kc].astype(F32))[:HEAD].astype(BF16)
        return 0

    lax.fori_loop(0, 8, turn_keys, 0)
    for i in (1, 3, 2):
        got(f"st{i}", stat_in.at[i])
    all_top = top
    for i in range(1, 4):
        all_top = jnp.maximum(all_top, stat_in[i, 0])
    up = jnp.exp2(top - all_top)
    total = total * up
    mixed = mixed * up
    for i in range(1, 4):
        up = jnp.exp2(stat_in[i, 0] - all_top)
        total = total + stat_in[i, 1] * up
        mixed = mixed + stat_in[i, 2] * up
    inverse = 1.0 / total
    delta[...] = mixed * inverse
    for kc in range(8):
        fac[kc] = jnp.exp2(tile_top[kc] - all_top) * inverse

    def step_of(k):
        return jnp.where(k % 2 == 1, (k + 1) // 2, (16 - k // 2) % 16)

    def owner(q, d):
        return dev(x, (y - 2 * c - q + 4) % 4, (z + d) % 16, y % 2)

    def ways(k):
        d = step_of(k)
        rho = jnp.where(k == 0, jnp.where(c == 0, 12, 4), (d + jnp.where(k % 2 == 1, 12, 4)) % 16)
        slot = jnp.where(k == 0, 3, 3 - (k + 1) // 2)
        flag = ((z + d) % 16) // 8 == home
        copies = []
        for q in range(2):
            copies.append(
                (
                    flag & jnp.logical_not(mine & (k == 0)) if q == 0 else flag,
                    pltpu.make_async_remote_copy(
                        src_ref=l1s.at[k, q], dst_ref=fin.at[k], send_sem=f_s.at[k, q],
                        recv_sem=f_r.at[k], device_id=owner(q, d), device_id_type=MESH,
                    ),
                )
            )
        copies.append(
            (
                jnp.logical_not(flag),
                pltpu.make_async_remote_copy(
                    src_ref=l1s.at[k], dst_ref=relay.at[slot], send_sem=r_s.at[k],
                    recv_sem=r_r.at[slot], device_id=on_z(rho), device_id_type=MESH,
                ),
            )
        )
        return copies

    def give(k):
        pltpu.make_async_copy(sbr.at[k], sbr.at[k], sb_r.at[k]).wait()
        l1s[k] = (own[k] + sbr[k].astype(F32)).astype(BF16)
        for flag, copy in ways(k):
            pl.when(flag)(copy.start)

    def share(k):
        return pltpu.make_async_remote_copy(
            src_ref=sbs.at[k], dst_ref=sbr.at[k], send_sem=sb_s.at[k], recv_sem=sb_r.at[k],
            device_id=sib, device_id_type=MESH,
        )

    def packed(rows):
        rows = rows.reshape(2, TOK, WIDE)
        return jnp.concatenate([rows[:, :32], rows[:, 32:]], axis=2)

    def key_group(k, _):
        kc = (zl + step_of(k)) % 8

        def rows_step(rt, dkv):
            p = prob[rt, kc] * fac[kc, pl.ds(rt, 1)]
            ds = (p * (grad[rt, kc] - delta[pl.ds(rt, 1)])).astype(BF16)
            dkv = dkv + dot(p.astype(BF16), wg[rt]) + dot(ds, wq[rt])
            dqt[rt] += dot(kt[kc], ds)
            return dkv

        dkf[...] = lax.fori_loop(0, 8, rows_step, jnp.zeros((RT, WIDE), F32), unroll=8)
        sbs[k] = packed(dkf[pl.ds(pl.multiple_of(128 * (1 - c), 128), 128)]).astype(BF16)
        own[k] = packed(dkf[pl.ds(pl.multiple_of(128 * c, 128), 128)])
        share(k).start()

        @pl.when(k >= 2)
        def _():
            give(k - 2)

        return 0

    lax.fori_loop(0, 8, key_group, 0)
    give(6)

    def row_ways(i, j):
        return pltpu.make_async_remote_copy(
            src_ref=dqb.at[i, j], dst_ref=dqr.at[i, y], send_sem=dq_s.at[i, j],
            recv_sem=dq_r.at[i, j],
            device_id=dev((x + i) % 4, (y - j + 4) % 4, z, c), device_id_type=MESH,
        )

    def rows_out(n, _):
        i = jnp.where(n == 0, 2, jnp.where(n == 1, 1, jnp.where(n == 2, 3, 0)))
        pair = dqt[pl.ds(((x + i) % 4) * 2, 2)].reshape(WIDE, RT)
        rows = (jnp.transpose(pair) * SCALE).reshape(4, TOK, WIDE)
        dqb[i] = jnp.concatenate([rows[:, :32], rows[:, 32:]], axis=2).astype(BF16)
        for j in (2, 1, 3):
            row_ways(i, j).start()
        pl.when(i > 0)(row_ways(i, 0).start)
        return 0

    lax.fori_loop(0, 4, rows_out, 0)
    dqr[0, y] = dqb[0, 0]

    pltpu.make_async_copy(sbr.at[7], sbr.at[7], sb_r.at[7]).wait()
    total = own[7] + sbr[7].astype(F32)
    for k in range(3):
        pltpu.make_async_copy(relay.at[k], relay.at[k], r_r.at[k]).wait()
        total = total + relay[k].astype(F32)
    ahead = ((z - 8 * home + 16 + 12) % 16) < 8
    fourth = ahead == (c == 0)
    dks[...] = total

    @pl.when(fourth)
    def _():
        pltpu.make_async_copy(relay.at[3], relay.at[3], r_r.at[3]).wait()
        dks[...] += relay[3].astype(F32)

    l1s[7] = dks[...].astype(BF16)
    side = jnp.where(ahead, 0, 1)
    forward = [
        pltpu.make_async_remote_copy(
            src_ref=l1s.at[7, q], dst_ref=fwd.at[side], send_sem=f_s.at[7, q],
            recv_sem=w_r.at[side], device_id=owner(q, jnp.where(ahead, 12, 4)),
            device_id_type=MESH,
        )
        for q in range(2)
    ]
    for copy in forward:
        copy.start()

    @pl.when(mine)
    def _():
        fin[0] = l1s[0, 0]

    def rows_sum(j, _):
        gs = (y + j) % 4

        @pl.when(j > 0)
        def _():
            pltpu.make_async_copy(dqr.at[0, gs], dqr.at[0, gs], dq_r.at[0, j]).wait()

        for i in (1, 3, 2):
            pltpu.make_async_copy(dqr.at[i, gs], dqr.at[i, gs], dq_r.at[i, j]).wait()
        total = dqr[0, gs].astype(F32)
        for i in range(1, 4):
            total = total + dqr[i, gs].astype(F32)
        dq_out[gs, :32] = total[:, :WIDE].astype(BF16)
        dq_out[gs, 32:] = total[:, WIDE:].astype(BF16)
        return 0

    lax.fori_loop(0, 4, rows_sum, 0)

    @pl.when(jnp.logical_not(mine))
    def _():
        pltpu.make_async_copy(fin.at[0], fin.at[0], f_r.at[0]).wait()

    total = fin[0].astype(F32)
    for k in range(1, 7):
        pltpu.make_async_copy(fin.at[k], fin.at[k], f_r.at[k]).wait()
        total = total + fin[k].astype(F32)
    for side in range(2):
        pltpu.make_async_copy(fwd.at[side], fwd.at[side], w_r.at[side]).wait()
        total = total + fwd[side].astype(F32)
    left = lax.broadcasted_iota(jnp.int32, (32, WIDE), 1) < HEAD
    scale = jnp.where(left, SCALE, 1.0)
    dkv_out[:32] = (total[:, :WIDE] * scale).astype(BF16)
    dkv_out[32:] = (total[:, WIDE:] * scale).astype(BF16)
    for copy in sent:
        copy.wait_send()
    for copy in forward:
        copy.wait_send()
    for n in range(8):
        pltpu.make_async_copy(kva.at[0, 0], kva.at[0, 0], send_sem.at[names[f"s{n}"]]).wait()

    def ended(k, _):
        share(k).wait_send()

        @pl.when(k < 7)
        def _():
            for flag, copy in ways(k):
                pl.when(flag)(copy.wait_send)

        return 0

    lax.fori_loop(0, 8, ended, 0)

    def rows_ended(i, _):
        for j in range(1, 4):
            row_ways(i, j).wait_send()
        pl.when(i > 0)(row_ways(i, 0).wait_send)
        return 0

    lax.fori_loop(0, 4, rows_ended, 0)


def per_device(query_matrix, key_matrix, value_matrix, output_gradient, stripe_map):
    vmem = pl.BlockSpec(memory_space=pltpu.VMEM)
    dma = pltpu.SemaphoreType.DMA
    dq, dkv = pl.pallas_call(
        kernel,
        out_shape=[
            jax.ShapeDtypeStruct((4, TOK, WIDE), BF16),
            jax.ShapeDtypeStruct((TOK, WIDE), BF16),
        ],
        in_specs=[pl.BlockSpec(memory_space=pltpu.SMEM)] + [vmem] * 4,
        out_specs=[vmem, vmem],
        scratch_shapes=[
            pltpu.VMEM((4, TOK, 2 * WIDE), BF16),
            pltpu.VMEM((4, 32, 2 * WIDE), BF16),
            pltpu.VMEM((4, 4, TOK, 2 * WIDE), BF16),
            pltpu.VMEM((2, 8, 4, 16, 2 * WIDE), BF16),
            pltpu.VMEM((8, RT, WIDE), BF16),
            pltpu.VMEM((8, HEAD, RT), BF16),
            pltpu.VMEM((8, RT, WIDE), BF16),
            pltpu.VMEM((8, RT, WIDE), BF16),
            pltpu.VMEM((8, 8, RT, RT), F32),
            pltpu.VMEM((8, 8, RT, RT), F32),
            pltpu.VMEM((8, 8, RT), F32),
            pltpu.VMEM((8, 8, RT), F32),
            pltpu.VMEM((8, 8, RT), F32),
            pltpu.VMEM((3, 8, RT), F32),
            pltpu.VMEM((4, 3, 8, RT), F32),
            pltpu.VMEM((8, 8, RT), F32),
            pltpu.VMEM((8, RT), F32),
            pltpu.VMEM((8, HEAD, RT), F32),
            pltpu.VMEM((RT, WIDE), F32),
            pltpu.VMEM((8, 2, 32, 2 * WIDE), F32),
            pltpu.VMEM((8, 2, 32, 2 * WIDE), BF16),
            pltpu.VMEM((8, 2, 32, 2 * WIDE), BF16),
            pltpu.VMEM((8, 2, 32, 2 * WIDE), BF16),
            pltpu.VMEM((4, 2, 32, 2 * WIDE), BF16),
            pltpu.VMEM((7, 32, 2 * WIDE), BF16),
            pltpu.VMEM((2, 32, 2 * WIDE), BF16),
            pltpu.VMEM((2, 32, 2 * WIDE), F32),
            pltpu.VMEM((4, 4, 32, 2 * WIDE), BF16),
            pltpu.VMEM((4, 4, 32, 2 * WIDE), BF16),
            dma((2,)), dma((N_SEM,)), dma((N_SEM,)),
            dma((8, 2)), dma((7,)), dma((7,)), dma((4,)), dma((2,)),
            dma((8,)), dma((8,)), dma((4, 4)), dma((4, 4)),
        ],
        compiler_params=pltpu.CompilerParams(
            collective_id=0, has_side_effects=True, vmem_limit_bytes=50 * 2**20
        ),
    )(
        stripe_map,
        query_matrix.transpose(1, 0, 2),
        output_gradient.transpose(1, 0, 2),
        key_matrix,
        value_matrix,
    )
    return dq.transpose(1, 0, 2), dkv[:, :HEAD], dkv[:, HEAD:]


def solution(mesh):
    return jax.shard_map(
        per_device,
        mesh=mesh,
        in_specs=(
            P(("blk", "uly"), None, "tp"),
            P(("blk", "uly"), None),
            P(("blk", "uly"), None),
            P(("blk", "uly"), None, "tp"),
            P(),
        ),
        out_specs=(P(("blk", "uly"), None, "tp"), P(("blk", "uly"), "tp"), P(("blk", "uly"), "tp")),
        check_vma=False,
    )
```

```python
import jax
import jax.numpy as jnp
from jax import lax
from jax.experimental import pallas as pl
from jax.experimental.pallas import tpu as pltpu
from jax.sharding import PartitionSpec as P

HEAD = 96
WIDE = 2 * HEAD
TOK = 64
RT = 256
LOG2E = 1.4426950408889634
SCALE = HEAD**-0.5
SCALE2 = SCALE * LOG2E
HIDE = -1e30
FLOOR = -1e29
F32 = jnp.float32
BF16 = jnp.bfloat16
MESH = pl.DeviceIdType.MESH
NT = (((1,), (1,)), ((), ()))
N_SEM = 96


def dot(a, b):
    return jnp.dot(a, b, preferred_element_type=F32)


def kernel(
    stripe, q_in, g_in, k_in, v_in, dq_out, dkv_out,
    qg, kv, qga, kva, kvu, kt, wq, wg, prob, grad,
    tile_top, tile_sum, tile_mix, stat, stat_in, fac, delta,
    dqt, dkf, own, sbs, sbr, l1s, land, l2s, fin, dqb, dqr,
    loc_sem, send_sem, recv_sem, f_s, f_r, l_s, l_r, sb_s, sb_r, dq_s, dq_r,
):
    b, y, t = lax.axis_index("blk"), lax.axis_index("uly"), lax.axis_index("tp")
    x, zl = b // 8, b % 8
    h, c = t // 2, t % 2
    z = h * 8 + zl

    def dev(x_, y_, z_, c_):
        return (x_ * 8 + z_ % 8, y_, (z_ // 8) * 2 + c_)

    def on_x(i):
        return dev((x + i) % 4, y, z, c)

    def on_y(j):
        return dev(x, (y + j) % 4, z, c)

    def on_z(d):
        return dev(x, y, (z + d) % 16, c)

    sib = dev(x, y, z, 1 - c)
    zsteps = (0, 1, 15, 2, 14, 3, 13, jnp.where(c == 0, 4, 12))
    sent = []
    names = {}

    def send(name, src, dst, to):
        n = names.setdefault(name, len(names))
        copy = pltpu.make_async_remote_copy(
            src_ref=src, dst_ref=dst, send_sem=send_sem.at[n], recv_sem=recv_sem.at[n],
            device_id=to, device_id_type=MESH,
        )
        copy.start()
        sent.append(copy)

    def got(name, ref):
        pltpu.make_async_copy(ref, ref, recv_sem.at[names[name]]).wait()

    barrier = pltpu.get_barrier_semaphore()
    peers = [dev((x + i) % 4, (y + j) % 4, z, c) for i in range(4) for j in range(4) if i or j]
    peers += [on_z(d) for d in (1, 15, 2, 14)]
    peers += [dev(x, (y + j) % 4, (z + d) % 16, c) for d in (3, 13, 4, 12) for j in range(4)]
    peers += [sib]

    def greet(to):
        pl.semaphore_signal(barrier, inc=1, device_id=to, device_id_type=MESH)

    for to in peers:
        greet(to)
    home = y // 2
    mine = (c == 0) & (y % 2 == 0) & (h == home)
    for hs in range(2):

        @pl.when(jnp.logical_not(mine & (h == hs)))
        def _():
            greet(dev(x, t, hs * 8 + zl, ((t - y + 4) % 4) // 2))

    for g in range(4):
        part = slice(g * HEAD, (g + 1) * HEAD)
        kv[g] = jnp.concatenate(
            [k_in[:32, part], v_in[:32, part], k_in[32:, part], v_in[32:, part]], axis=1
        )
        qs, gs = q_in[g], g_in[g]
        qg[g] = jnp.concatenate(
            [qs[:, :HEAD], gs[:, :HEAD], qs[:, HEAD:], gs[:, HEAD:]], axis=1
        )
    pl.semaphore_wait(barrier, len(peers) + 2 - jnp.where(mine, 1, 0))

    half = pl.ds(pl.multiple_of(16 * c, 16), 16)

    def send_kv(n, j):
        send(
            f"k{n}_{j}", kv.at[(y + j) % 4, half], kva.at[c, zl, j],
            dev(x, (y + j) % 4, (z + zsteps[n]) % 16, c),
        )

    loc_kv = pltpu.make_async_copy(kv.at[y, half], kva.at[c, zl, 0], loc_sem.at[0])
    loc_kv.start()
    loc_qg = pltpu.make_async_copy(qg.at[y], qga.at[x, 0], loc_sem.at[1])
    loc_qg.start()
    for j in (1, 3, 2):
        send_kv(0, j)
    for j in (1, 3, 2):
        send(f"qy{j}", qg.at[(y + j) % 4], qga.at[x, j], on_y(j))
    for i in (1, 3):
        send(f"x{i}_0", qg.at[y], qga.at[x, 0], on_x(i))
    for n in (7, 5, 6):
        for j in (0, 1, 3, 2):
            send_kv(n, j)
    for n in range(1, 5):
        send_kv(n, 0)
    for j in (0, 1, 3, 2):
        send(
            f"x2_{j}", qg.at[(y + j) % 4], qga.at[x, j],
            dev((x + 2) % 4, (y + j) % 4, z, c),
        )
    rest = pl.ds(1, 3)

    def share_kv(n):
        zs = (zl + 16 - zsteps[n]) % 8
        if 0 < n < 5:
            got(f"k{n}_0", kva.at[c, zs, 0])
            got(f"k{n}_r", kva.at[c, zs, rest])
        else:
            for j in range(4):
                if n or j:
                    got(f"k{n}_{j}", kva.at[c, zs, j])
        if n == 0:
            for d in range(1, 5):
                send(f"k{d}_r", kva.at[c, zl, rest], kva.at[c, zl, rest], on_z(zsteps[d]))
        send(f"s{n}", kva.at[c, zs], kva.at[c, zs], sib)

    loc_kv.wait()
    share_kv(0)
    for j in (1, 3, 2):
        got(f"qy{j}", qga.at[x, j])
        for i in (1, 3):
            send(f"x{i}_{j}", qga.at[x, j], qga.at[x, j], on_x(i))

    lane = lax.broadcasted_iota(jnp.int32, (1, RT), 1)
    sub = lax.broadcasted_iota(jnp.int32, (TOK, RT), 0)
    low_lanes = lax.broadcasted_iota(jnp.int32, (RT, WIDE), 1) < HEAD

    def order(n):
        return (zl + jnp.where(n % 2 == 1, 8 - (n + 1) // 2, n // 2)) % 8

    def unpack(n):
        zs = order(n)
        for hf in range(2):
            for j in range(4):
                v = kva[hf, zs, j]
                kvu[zs, TOK * j + 16 * hf : TOK * j + 16 * hf + 16, :] = v[:, :WIDE]
                kvu[zs, TOK * j + 32 + 16 * hf : TOK * j + 48 + 16 * hf, :] = v[:, WIDE:]

    def rows_in(xs):
        both = qga[xs].reshape(RT, 2 * WIDE)
        zero = jnp.zeros((RT, WIDE), BF16)
        for m in range(2):
            part = both[:, m * WIDE : (m + 1) * WIDE]
            wq[xs * 2 + m] = jnp.where(low_lanes, part, zero)
            wg[xs * 2 + m] = jnp.where(low_lanes, zero, part)

    def block_of(xs, zs, j):
        return stripe[(xs * 8 + zs) * 4 + (y - j + 4) % 4]

    def rows_of(xs):
        out = jnp.zeros((1, RT), jnp.int32)
        for j in range(4):
            out = jnp.where(lane // TOK == j, block_of(xs, zl, j), out)
        return out

    def tile(xs, row_block, kc, diagonal=False):
        for m in range(2):
            rt = xs * 2 + m
            s = lax.dot_general(kvu[kc], wq[rt], NT, preferred_element_type=F32) * SCALE2
            pg = lax.dot_general(kvu[kc], wg[rt], NT, preferred_element_type=F32)
            pieces, biases = [], []
            top = jnp.full((8, RT), FLOOR, F32)
            for j in range(4):
                piece = s[TOK * j : TOK * (j + 1)]
                key_block = block_of(x, kc, j)
                if diagonal:
                    seen = sub + key_block * TOK <= row_block * TOK + lane % TOK
                    piece = jnp.where(seen, piece, HIDE)
                    bias = jnp.zeros((1, RT), F32)
                else:
                    bias = jnp.where(key_block > row_block, HIDE, 0.0)
                top = jnp.maximum(top, jnp.max(piece.reshape(8, 8, RT), axis=0) + bias)
                pieces.append(piece)
                biases.append(bias)
            top = jnp.max(top, axis=0, keepdims=True)
            total = jnp.zeros((8, RT), F32)
            mixed = jnp.zeros((8, RT), F32)
            for j in range(4):
                e = jnp.exp2(pieces[j] - (top - biases[j]))
                prob[rt, kc, TOK * j : TOK * (j + 1)] = e
                total = total + jnp.sum(e.reshape(8, 8, RT), axis=0)
                mixed = mixed + jnp.sum(
                    (e * pg[TOK * j : TOK * (j + 1)]).reshape(8, 8, RT), axis=0
                )
            grad[rt, kc] = pg
            tile_top[kc, pl.ds(rt, 1)] = top
            tile_sum[kc, pl.ds(rt, 1)] = jnp.sum(total, axis=0, keepdims=True)
            tile_mix[kc, pl.ds(rt, 1)] = jnp.sum(mixed, axis=0, keepdims=True)

    def tiles(xs, lo, count, turns=1):
        row_block = rows_of(xs)

        def step(turn, _):
            for n in range(count):
                tile(xs, row_block, order(lo + turn * count + n))
            return 0

        lax.fori_loop(0, turns, step, 0)

    loc_qg.wait()
    rows_in(x)
    got("s0", kva.at[1 - c, zl])
    unpack(0)
    tile(x, rows_of(x), zl, True)

    def take_keys(lo, count):
        for n in range(lo, lo + count):
            share_kv(n)
        for n in range(lo, lo + count):
            got(f"s{n}", kva.at[1 - c, order(n)])
            unpack(n)

    def take_rows(i):
        xs = (x - i + 4) % 4
        for j in range(4):
            got(f"x{i}_{j}", qga.at[xs, j])
        rows_in(xs)
        return xs

    take_keys(1, 4)
    tiles(x, 1, 4)
    across = take_rows(2)
    tiles(across, 0, 4)
    take_keys(5, 3)
    tiles(x, 5, 3)
    tiles(across, 4, 4)
    for i in (1, 3):
        tiles(take_rows(i), 0, 4, 2)

    top = tile_top[0]
    for kc in range(1, 8):
        top = jnp.maximum(top, tile_top[kc])
    total = jnp.zeros((8, RT), F32)
    mixed = jnp.zeros((8, RT), F32)
    for kc in range(8):
        up = jnp.exp2(tile_top[kc] - top)
        total = total + tile_sum[kc] * up
        mixed = mixed + tile_mix[kc] * up
    stat[0] = top
    stat[1] = total
    stat[2] = mixed
    for i in (2, 1, 3):
        send(f"st{i}", stat, stat_in.at[i], on_x(i))
    dqt[...] = jnp.zeros_like(dqt)

    def turn_keys(kc, _):
        kt[kc] = jnp.transpose(kvu[kc].astype(F32))[:HEAD].astype(BF16)
        return 0

    lax.fori_loop(0, 8, turn_keys, 0)
    for i in (1, 3, 2):
        got(f"st{i}", stat_in.at[i])
    all_top = top
    for i in range(1, 4):
        all_top = jnp.maximum(all_top, stat_in[i, 0])
    up = jnp.exp2(top - all_top)
    total = total * up
    mixed = mixed * up
    for i in range(1, 4):
        up = jnp.exp2(stat_in[i, 0] - all_top)
        total = total + stat_in[i, 1] * up
        mixed = mixed + stat_in[i, 2] * up
    inverse = 1.0 / total
    delta[...] = mixed * inverse
    for kc in range(8):
        fac[kc] = jnp.exp2(tile_top[kc] - all_top) * inverse

    def step_of(k):
        return jnp.where(k % 2 == 1, (7 - k) // 2, 4 + k // 2)

    def give(k):
        d = jnp.where(k == 0, jnp.where(c == 0, 2, 14), 0)
        d = jnp.where((k == 1) | (k == 5), 1, jnp.where((k == 2) | (k == 6), 15, d))
        d = jnp.where(k == 3, 2, jnp.where(k == 4, 14, d))
        return pltpu.make_async_remote_copy(
            src_ref=l1s.at[k], dst_ref=land.at[k], send_sem=l_s.at[k], recv_sem=l_r.at[k],
            device_id=on_z(d), device_id_type=MESH,
        )

    def landed(k):
        pltpu.make_async_copy(land.at[k], land.at[k], l_r.at[k]).wait()

    def both(k):
        pltpu.make_async_copy(sbr.at[k], sbr.at[k], sb_r.at[k]).wait()
        return own[k] + sbr[k].astype(F32)

    def share(k):
        return pltpu.make_async_remote_copy(
            src_ref=sbs.at[k], dst_ref=sbr.at[k], send_sem=sb_s.at[k], recv_sem=sb_r.at[k],
            device_id=sib, device_id_type=MESH,
        )

    def packed(rows):
        rows = rows.reshape(2, TOK, WIDE)
        return jnp.concatenate([rows[:, :32], rows[:, 32:]], axis=2)

    def key_group(k, _):
        kc = (zl + step_of(k)) % 8

        def rows_step(rt, dkv):
            p = prob[rt, kc] * fac[kc, pl.ds(rt, 1)]
            ds = (p * (grad[rt, kc] - delta[pl.ds(rt, 1)])).astype(BF16)
            dkv = dkv + dot(p.astype(BF16), wg[rt]) + dot(ds, wq[rt])
            dqt[rt] += dot(kt[kc], ds)
            return dkv

        dkf[...] = lax.fori_loop(0, 8, rows_step, jnp.zeros((RT, WIDE), F32), unroll=8)
        sbs[k] = packed(dkf[pl.ds(pl.multiple_of(128 * (1 - c), 128), 128)]).astype(BF16)
        own[k] = packed(dkf[pl.ds(pl.multiple_of(128 * c, 128), 128)])
        share(k).start()

        @pl.when((k >= 2) & ((k < 5) | (k == 7)))
        def _():
            l1s[k - 2] = both(k - 2).astype(BF16)
            give(k - 2).start()

        return 0

    lax.fori_loop(0, 8, key_group, 0)
    l1s[6] = both(6).astype(BF16)
    give(6).start()
    landed(0)
    for k in (3, 4):
        landed(k - 2)
        far = land[0].astype(F32)
        total = both(k) + land[k - 2].astype(F32)
        l1s[k] = (total + jnp.where(c == k - 3, far, jnp.zeros_like(far))).astype(BF16)
        give(k).start()

    def row_ways(i, j):
        return pltpu.make_async_remote_copy(
            src_ref=dqb.at[i, j], dst_ref=dqr.at[i, y], send_sem=dq_s.at[i, j],
            recv_sem=dq_r.at[i, j],
            device_id=dev((x + i) % 4, (y - j + 4) % 4, z, c), device_id_type=MESH,
        )

    def rows_out(n, _):
        i = jnp.where(n == 0, 2, jnp.where(n == 1, 1, jnp.where(n == 2, 3, 0)))
        pair = dqt[pl.ds(((x + i) % 4) * 2, 2)].reshape(WIDE, RT)
        rows = (jnp.transpose(pair) * SCALE).reshape(4, TOK, WIDE)
        dqb[i] = jnp.concatenate([rows[:, :32], rows[:, 32:]], axis=2).astype(BF16)
        for j in (2, 1, 3):
            row_ways(i, j).start()
        pl.when(i > 0)(row_ways(i, 0).start)
        return 0

    lax.fori_loop(0, 4, rows_out, 0)
    dqr[0, y] = dqb[0, 0]

    total = both(7)
    for k in (5, 6, 3, 4):
        landed(k)
        total = total + land[k].astype(F32)
    l2s[...] = total.astype(BF16)
    forward = []
    for q in range(2):
        copy = pltpu.make_async_remote_copy(
            src_ref=l2s.at[q], dst_ref=fin.at[h], send_sem=f_s.at[q], recv_sem=f_r.at[h],
            device_id=dev(x, (y - 2 * c - q + 4) % 4, 8 * home + zl, y % 2), device_id_type=MESH,
        )
        if q:
            copy.start()
        else:
            pl.when(jnp.logical_not(mine))(copy.start)
        forward.append(copy)

    @pl.when(mine)
    def _():
        fin[h] = l2s[0]

    def rows_sum(j, _):
        gs = (y + j) % 4

        @pl.when(j > 0)
        def _():
            pltpu.make_async_copy(dqr.at[0, gs], dqr.at[0, gs], dq_r.at[0, j]).wait()

        for i in (1, 3, 2):
            pltpu.make_async_copy(dqr.at[i, gs], dqr.at[i, gs], dq_r.at[i, j]).wait()
        total = dqr[0, gs].astype(F32)
        for i in range(1, 4):
            total = total + dqr[i, gs].astype(F32)
        dq_out[gs, :32] = total[:, :WIDE].astype(BF16)
        dq_out[gs, 32:] = total[:, WIDE:].astype(BF16)
        return 0

    lax.fori_loop(0, 4, rows_sum, 0)

    for hs in range(2):

        @pl.when(jnp.logical_not(mine & (h == hs)))
        def _():
            pltpu.make_async_copy(fin.at[hs], fin.at[hs], f_r.at[hs]).wait()

    total = fin[0].astype(F32) + fin[1].astype(F32)
    left = lax.broadcasted_iota(jnp.int32, (32, WIDE), 1) < HEAD
    scale = jnp.where(left, SCALE, 1.0)
    dkv_out[:32] = (total[:, :WIDE] * scale).astype(BF16)
    dkv_out[32:] = (total[:, WIDE:] * scale).astype(BF16)
    for copy in sent:
        copy.wait_send()
    forward[1].wait_send()
    pl.when(jnp.logical_not(mine))(forward[0].wait_send)
    def ended(k, _):
        share(k).wait_send()

        pl.when(k < 7)(give(jnp.minimum(k, 6)).wait_send)
        return 0

    lax.fori_loop(0, 8, ended, 0)

    def rows_ended(i, _):
        for j in range(1, 4):
            row_ways(i, j).wait_send()
        pl.when(i > 0)(row_ways(i, 0).wait_send)
        return 0

    lax.fori_loop(0, 4, rows_ended, 0)


def per_device(query_matrix, key_matrix, value_matrix, output_gradient, stripe_map):
    vmem = pl.BlockSpec(memory_space=pltpu.VMEM)
    dma = pltpu.SemaphoreType.DMA
    dq, dkv = pl.pallas_call(
        kernel,
        out_shape=[
            jax.ShapeDtypeStruct((4, TOK, WIDE), BF16),
            jax.ShapeDtypeStruct((TOK, WIDE), BF16),
        ],
        in_specs=[pl.BlockSpec(memory_space=pltpu.SMEM)] + [vmem] * 4,
        out_specs=[vmem, vmem],
        scratch_shapes=[
            pltpu.VMEM((4, TOK, 2 * WIDE), BF16),
            pltpu.VMEM((4, 32, 2 * WIDE), BF16),
            pltpu.VMEM((4, 4, TOK, 2 * WIDE), BF16),
            pltpu.VMEM((2, 8, 4, 16, 2 * WIDE), BF16),
            pltpu.VMEM((8, RT, WIDE), BF16),
            pltpu.VMEM((8, HEAD, RT), BF16),
            pltpu.VMEM((8, RT, WIDE), BF16),
            pltpu.VMEM((8, RT, WIDE), BF16),
            pltpu.VMEM((8, 8, RT, RT), F32),
            pltpu.VMEM((8, 8, RT, RT), F32),
            pltpu.VMEM((8, 8, RT), F32),
            pltpu.VMEM((8, 8, RT), F32),
            pltpu.VMEM((8, 8, RT), F32),
            pltpu.VMEM((3, 8, RT), F32),
            pltpu.VMEM((4, 3, 8, RT), F32),
            pltpu.VMEM((8, 8, RT), F32),
            pltpu.VMEM((8, RT), F32),
            pltpu.VMEM((8, HEAD, RT), F32),
            pltpu.VMEM((RT, WIDE), F32),
            pltpu.VMEM((8, 2, 32, 2 * WIDE), F32),
            pltpu.VMEM((8, 2, 32, 2 * WIDE), BF16),
            pltpu.VMEM((8, 2, 32, 2 * WIDE), BF16),
            pltpu.VMEM((7, 2, 32, 2 * WIDE), BF16),
            pltpu.VMEM((7, 2, 32, 2 * WIDE), BF16),
            pltpu.VMEM((2, 32, 2 * WIDE), BF16),
            pltpu.VMEM((2, 32, 2 * WIDE), BF16),
            pltpu.VMEM((4, 4, 32, 2 * WIDE), BF16),
            pltpu.VMEM((4, 4, 32, 2 * WIDE), BF16),
            dma((2,)), dma((N_SEM,)), dma((N_SEM,)),
            dma((2,)), dma((2,)), dma((7,)), dma((7,)),
            dma((8,)), dma((8,)), dma((4, 4)), dma((4, 4)),
        ],
        compiler_params=pltpu.CompilerParams(
            collective_id=0, has_side_effects=True, vmem_limit_bytes=50 * 2**20
        ),
    )(
        stripe_map,
        query_matrix.transpose(1, 0, 2),
        output_gradient.transpose(1, 0, 2),
        key_matrix,
        value_matrix,
    )
    return dq.transpose(1, 0, 2), dkv[:, :HEAD], dkv[:, HEAD:]


def solution(mesh):
    return jax.shard_map(
        per_device,
        mesh=mesh,
        in_specs=(
            P(("blk", "uly"), None, "tp"),
            P(("blk", "uly"), None),
            P(("blk", "uly"), None),
            P(("blk", "uly"), None, "tp"),
            P(),
        ),
        out_specs=(P(("blk", "uly"), None, "tp"), P(("blk", "uly"), "tp"), P(("blk", "uly"), "tp")),
        check_vma=False,
    )
```

```python
import jax
import jax.numpy as jnp
from jax import lax
from jax.experimental import pallas as pl
from jax.experimental.pallas import tpu as pltpu
from jax.sharding import PartitionSpec as P

HEAD = 96
WIDE = 2 * HEAD
TOK = 64
RT = 256
LOG2E = 1.4426950408889634
SCALE = HEAD**-0.5
SCALE2 = SCALE * LOG2E
HIDE = -1e30
FLOOR = -1e29
F32 = jnp.float32
BF16 = jnp.bfloat16
MESH = pl.DeviceIdType.MESH
NT = (((1,), (1,)), ((), ()))
N_SEM = 96


def dot(a, b):
    return jnp.dot(a, b, preferred_element_type=F32)


def kernel(
    stripe, q_in, g_in, k_in, v_in, dq_out, dkv_out,
    qg, kv, qga, kva, kvu, kt, wq, wg, prob, grad,
    tile_top, tile_sum, tile_mix, stat, stat_in, fac, delta,
    dqt, dkf, own, sbs, sbr, l1s, land, l2s, fin, dqb, dqr,
    loc_sem, send_sem, recv_sem, f_s, f_r, l_s, l_r, sb_s, sb_r, dq_s, dq_r,
):
    b, y, t = lax.axis_index("blk"), lax.axis_index("uly"), lax.axis_index("tp")
    x, zl = b // 8, b % 8
    h, c = t // 2, t % 2
    z = h * 8 + zl

    def dev(x_, y_, z_, c_):
        return (x_ * 8 + z_ % 8, y_, (z_ // 8) * 2 + c_)

    def on_x(i):
        return dev((x + i) % 4, y, z, c)

    def on_y(j):
        return dev(x, (y + j) % 4, z, c)

    def on_z(d):
        return dev(x, y, (z + d) % 16, c)

    sib = dev(x, y, z, 1 - c)
    zsteps = (0, 1, 15, 2, 14, 3, 13, jnp.where(c == 0, 4, 12))
    sent = []
    names = {}

    def send(name, src, dst, to):
        n = names.setdefault(name, len(names))
        copy = pltpu.make_async_remote_copy(
            src_ref=src, dst_ref=dst, send_sem=send_sem.at[n], recv_sem=recv_sem.at[n],
            device_id=to, device_id_type=MESH,
        )
        copy.start()
        sent.append(copy)

    def got(name, ref):
        pltpu.make_async_copy(ref, ref, recv_sem.at[names[name]]).wait()

    barrier = pltpu.get_barrier_semaphore()
    peers = [dev((x + i) % 4, (y + j) % 4, z, c) for i in range(4) for j in range(4) if i or j]
    peers += [on_z(d) for d in (1, 15, 2, 14)]
    peers += [dev(x, (y + j) % 4, (z + d) % 16, c) for d in (3, 13, 4, 12) for j in range(4)]
    peers += [sib]

    def greet(to):
        pl.semaphore_signal(barrier, inc=1, device_id=to, device_id_type=MESH)

    for to in peers:
        greet(to)
    home = y // 2
    mine = (c == 0) & (y % 2 == 0) & (h == home)
    for hs in range(2):

        @pl.when(jnp.logical_not(mine & (h == hs)))
        def _():
            greet(dev(x, t, hs * 8 + zl, ((t - y + 4) % 4) // 2))

    for g in range(4):
        part = slice(g * HEAD, (g + 1) * HEAD)
        kv[g] = jnp.concatenate(
            [k_in[:32, part], v_in[:32, part], k_in[32:, part], v_in[32:, part]], axis=1
        )
        qs, gs = q_in[g], g_in[g]
        qg[g] = jnp.concatenate(
            [qs[:, :HEAD], gs[:, :HEAD], qs[:, HEAD:], gs[:, HEAD:]], axis=1
        )
    pl.semaphore_wait(barrier, len(peers) + 2 - jnp.where(mine, 1, 0))

    half = pl.ds(pl.multiple_of(16 * c, 16), 16)

    def send_kv(n, j):
        send(
            f"k{n}_{j}", kv.at[(y + j) % 4, half], kva.at[c, zl, j],
            dev(x, (y + j) % 4, (z + zsteps[n]) % 16, c),
        )

    loc_kv = pltpu.make_async_copy(kv.at[y, half], kva.at[c, zl, 0], loc_sem.at[0])
    loc_kv.start()
    loc_qg = pltpu.make_async_copy(qg.at[y], qga.at[x, 0], loc_sem.at[1])
    loc_qg.start()
    for j in (1, 3, 2):
        send_kv(0, j)
    for j in (1, 3, 2):
        send(f"qy{j}", qg.at[(y + j) % 4], qga.at[x, j], on_y(j))
    for i in (1, 3):
        send(f"x{i}_0", qg.at[y], qga.at[x, 0], on_x(i))
    for n in (7, 5, 6):
        for j in (0, 1, 3, 2):
            send_kv(n, j)
    for n in range(1, 5):
        send_kv(n, 0)
    for j in (0, 1, 3, 2):
        send(
            f"x2_{j}", qg.at[(y + j) % 4], qga.at[x, j],
            dev((x + 2) % 4, (y + j) % 4, z, c),
        )
    rest = pl.ds(1, 3)

    def share_kv(n):
        zs = (zl + 16 - zsteps[n]) % 8
        if 0 < n < 5:
            got(f"k{n}_0", kva.at[c, zs, 0])
            got(f"k{n}_r", kva.at[c, zs, rest])
        else:
            for j in range(4):
                if n or j:
                    got(f"k{n}_{j}", kva.at[c, zs, j])
        if n == 0:
            for d in range(1, 5):
                send(f"k{d}_r", kva.at[c, zl, rest], kva.at[c, zl, rest], on_z(zsteps[d]))
        send(f"s{n}", kva.at[c, zs], kva.at[c, zs], sib)

    loc_kv.wait()
    share_kv(0)
    for j in (1, 3, 2):
        got(f"qy{j}", qga.at[x, j])
        for i in (1, 3):
            send(f"x{i}_{j}", qga.at[x, j], qga.at[x, j], on_x(i))

    lane = lax.broadcasted_iota(jnp.int32, (1, RT), 1)
    sub = lax.broadcasted_iota(jnp.int32, (TOK, RT), 0)
    low_lanes = lax.broadcasted_iota(jnp.int32, (RT, WIDE), 1) < HEAD

    def order(n):
        return (zl + jnp.where(n % 2 == 1, 8 - (n + 1) // 2, n // 2)) % 8

    def unpack(n):
        zs = order(n)
        for hf in range(2):
            for j in range(4):
                v = kva[hf, zs, j]
                kvu[zs, TOK * j + 16 * hf : TOK * j + 16 * hf + 16, :] = v[:, :WIDE]
                kvu[zs, TOK * j + 32 + 16 * hf : TOK * j + 48 + 16 * hf, :] = v[:, WIDE:]

    def rows_in(xs):
        both = qga[xs].reshape(RT, 2 * WIDE)
        zero = jnp.zeros((RT, WIDE), BF16)
        for m in range(2):
            part = both[:, m * WIDE : (m + 1) * WIDE]
            wq[xs * 2 + m] = jnp.where(low_lanes, part, zero)
            wg[xs * 2 + m] = jnp.where(low_lanes, zero, part)

    def block_of(xs, zs, j):
        return stripe[(xs * 8 + zs) * 4 + (y - j + 4) % 4]

    def rows_of(xs):
        out = jnp.zeros((1, RT), jnp.int32)
        for j in range(4):
            out = jnp.where(lane // TOK == j, block_of(xs, zl, j), out)
        return out

    def tile(xs, row_block, kc, diagonal=False):
        for m in range(2):
            rt = xs * 2 + m
            s = lax.dot_general(kvu[kc], wq[rt], NT, preferred_element_type=F32) * SCALE2
            pg = lax.dot_general(kvu[kc], wg[rt], NT, preferred_element_type=F32)
            pieces, biases = [], []
            top = jnp.full((8, RT), FLOOR, F32)
            for j in range(4):
                piece = s[TOK * j : TOK * (j + 1)]
                key_block = block_of(x, kc, j)
                if diagonal:
                    seen = sub + key_block * TOK <= row_block * TOK + lane % TOK
                    piece = jnp.where(seen, piece, HIDE)
                    bias = jnp.zeros((1, RT), F32)
                else:
                    bias = jnp.where(key_block > row_block, HIDE, 0.0)
                top = jnp.maximum(top, jnp.max(piece.reshape(8, 8, RT), axis=0) + bias)
                pieces.append(piece)
                biases.append(bias)
            top = jnp.max(top, axis=0, keepdims=True)
            total = jnp.zeros((8, RT), F32)
            mixed = jnp.zeros((8, RT), F32)
            for j in range(4):
                e = jnp.exp2(pieces[j] - (top - biases[j]))
                prob[rt, kc, TOK * j : TOK * (j + 1)] = e
                total = total + jnp.sum(e.reshape(8, 8, RT), axis=0)
                mixed = mixed + jnp.sum(
                    (e * pg[TOK * j : TOK * (j + 1)]).reshape(8, 8, RT), axis=0
                )
            grad[rt, kc] = pg
            tile_top[kc, pl.ds(rt, 1)] = top
            tile_sum[kc, pl.ds(rt, 1)] = jnp.sum(total, axis=0, keepdims=True)
            tile_mix[kc, pl.ds(rt, 1)] = jnp.sum(mixed, axis=0, keepdims=True)

    def tiles(xs, lo, count, turns=1):
        row_block = rows_of(xs)

        def step(turn, _):
            for n in range(count):
                tile(xs, row_block, order(lo + turn * count + n))
            return 0

        lax.fori_loop(0, turns, step, 0)

    loc_qg.wait()
    rows_in(x)
    got("s0", kva.at[1 - c, zl])
    unpack(0)
    tile(x, rows_of(x), zl, True)

    def take_keys(lo, count):
        for n in range(lo, lo + count):
            share_kv(n)
        for n in range(lo, lo + count):
            got(f"s{n}", kva.at[1 - c, order(n)])
            unpack(n)

    def take_rows(i):
        xs = (x - i + 4) % 4
        for j in range(4):
            got(f"x{i}_{j}", qga.at[xs, j])
        rows_in(xs)
        return xs

    take_keys(1, 4)
    tiles(x, 1, 4)
    across = take_rows(2)
    tiles(across, 0, 4)
    take_keys(5, 3)
    tiles(x, 5, 3)
    tiles(across, 4, 4)

    for i in (1, 3):
        tiles(take_rows(i), 0, 4, 2)

    top = tile_top[0]
    for kc in range(1, 8):
        top = jnp.maximum(top, tile_top[kc])
    total = jnp.zeros((8, RT), F32)
    mixed = jnp.zeros((8, RT), F32)
    for kc in range(8):
        up = jnp.exp2(tile_top[kc] - top)
        total = total + tile_sum[kc] * up
        mixed = mixed + tile_mix[kc] * up
    stat[0] = top
    stat[1] = total
    stat[2] = mixed
    for i in (2, 1, 3):
        send(f"st{i}", stat, stat_in.at[i], on_x(i))

    def turn_keys(kc, _):
        kt[kc] = jnp.transpose(kvu[kc].astype(F32))[:HEAD].astype(BF16)
        return 0

    lax.fori_loop(0, 8, turn_keys, 0)
    for i in (1, 3, 2):
        got(f"st{i}", stat_in.at[i])
    all_top = top
    for i in range(1, 4):
        all_top = jnp.maximum(all_top, stat_in[i, 0])
    up = jnp.exp2(top - all_top)
    total = total * up
    mixed = mixed * up
    for i in range(1, 4):
        up = jnp.exp2(stat_in[i, 0] - all_top)
        total = total + stat_in[i, 1] * up
        mixed = mixed + stat_in[i, 2] * up
    inverse = 1.0 / total
    delta[...] = mixed * inverse
    for kc in range(8):
        fac[kc] = jnp.exp2(tile_top[kc] - all_top) * inverse

    def step_of(k):
        return jnp.where(k % 2 == 1, (7 - k) // 2, 4 + k // 2)

    def give(k):
        d = jnp.where(k == 0, jnp.where(c == 0, 2, 14), 0)
        d = jnp.where((k == 1) | (k == 5), 1, jnp.where((k == 2) | (k == 6), 15, d))
        d = jnp.where(k == 3, 2, jnp.where(k == 4, 14, d))
        return pltpu.make_async_remote_copy(
            src_ref=l1s.at[k], dst_ref=land.at[k], send_sem=l_s.at[k], recv_sem=l_r.at[k],
            device_id=on_z(d), device_id_type=MESH,
        )

    def landed(k):
        pltpu.make_async_copy(land.at[k], land.at[k], l_r.at[k]).wait()

    def both(k):
        pltpu.make_async_copy(sbr.at[k], sbr.at[k], sb_r.at[k]).wait()
        return own[k] + sbr[k].astype(F32)

    def share(k):
        return pltpu.make_async_remote_copy(
            src_ref=sbs.at[k], dst_ref=sbr.at[k], send_sem=sb_s.at[k], recv_sem=sb_r.at[k],
            device_id=sib, device_id_type=MESH,
        )

    def packed(rows):
        rows = rows.reshape(2, TOK, WIDE)
        return jnp.concatenate([rows[:, :32], rows[:, 32:]], axis=2)

    def key_group(k, _):
        kc = (zl + step_of(k)) % 8

        def rows_step(rt, dkv):
            p = prob[rt, kc] * fac[kc, pl.ds(rt, 1)]
            ds = p * (grad[rt, kc] - delta[pl.ds(rt, 1)])
            grad[rt, kc] = ds
            return dkv + dot(p.astype(BF16), wg[rt]) + dot(ds.astype(BF16), wq[rt])

        dkf[...] = lax.fori_loop(0, 8, rows_step, jnp.zeros((RT, WIDE), F32), unroll=8)
        sbs[k] = packed(dkf[pl.ds(pl.multiple_of(128 * (1 - c), 128), 128)]).astype(BF16)
        own[k] = packed(dkf[pl.ds(pl.multiple_of(128 * c, 128), 128)])
        share(k).start()

        @pl.when((k >= 2) & ((k < 5) | (k == 7)))
        def _():
            l1s[k - 2] = both(k - 2).astype(BF16)
            give(k - 2).start()

        return 0

    lax.fori_loop(0, 8, key_group, 0)
    l1s[6] = both(6).astype(BF16)
    give(6).start()

    def merge():
        landed(0)
        for k in (3, 4):
            landed(k - 2)
            far = land[0].astype(F32)
            total = both(k) + land[k - 2].astype(F32)
            l1s[k] = (total + jnp.where(c == k - 3, far, jnp.zeros_like(far))).astype(BF16)
            give(k).start()

    def row_ways(i, j):
        return pltpu.make_async_remote_copy(
            src_ref=dqb.at[i, j], dst_ref=dqr.at[i, y], send_sem=dq_s.at[i, j],
            recv_sem=dq_r.at[i, j],
            device_id=dev((x + i) % 4, (y - j + 4) % 4, z, c), device_id_type=MESH,
        )

    def rows_out(n, _):
        i = jnp.where(n == 0, 2, jnp.where(n == 1, 1, jnp.where(n == 2, 3, 0)))

        for m in range(2):
            rt = ((x + i) % 4) * 2 + m
            part = jnp.zeros((HEAD, RT), F32)
            for kc in range(8):
                part = part + dot(kt[kc], grad[rt, kc].astype(BF16))
            dqt[m] = part
        pair = dqt[...].reshape(WIDE, RT)
        rows = (jnp.transpose(pair) * SCALE).reshape(4, TOK, WIDE)
        dqb[i] = jnp.concatenate([rows[:, :32], rows[:, 32:]], axis=2).astype(BF16)
        for j in (2, 1, 3):
            row_ways(i, j).start()
        pl.when(i > 0)(row_ways(i, 0).start)
        return 0

    merge()
    lax.fori_loop(0, 4, rows_out, 0)
    dqr[0, y] = dqb[0, 0]

    total = both(7)
    for k in (5, 6, 3, 4):
        landed(k)
        total = total + land[k].astype(F32)
    l2s[...] = total.astype(BF16)
    forward = []
    for q in range(2):
        copy = pltpu.make_async_remote_copy(
            src_ref=l2s.at[q], dst_ref=fin.at[h], send_sem=f_s.at[q], recv_sem=f_r.at[h],
            device_id=dev(x, (y - 2 * c - q + 4) % 4, 8 * home + zl, y % 2), device_id_type=MESH,
        )
        if q:
            copy.start()
        else:
            pl.when(jnp.logical_not(mine))(copy.start)
        forward.append(copy)

    @pl.when(mine)
    def _():
        fin[h] = l2s[0]

    def rows_sum(j, _):
        gs = (y + j) % 4

        @pl.when(j > 0)
        def _():
            pltpu.make_async_copy(dqr.at[0, gs], dqr.at[0, gs], dq_r.at[0, j]).wait()

        for i in (1, 3, 2):
            pltpu.make_async_copy(dqr.at[i, gs], dqr.at[i, gs], dq_r.at[i, j]).wait()
        total = dqr[0, gs].astype(F32)
        for i in range(1, 4):
            total = total + dqr[i, gs].astype(F32)
        dq_out[gs, :32] = total[:, :WIDE].astype(BF16)
        dq_out[gs, 32:] = total[:, WIDE:].astype(BF16)
        return 0

    lax.fori_loop(0, 4, rows_sum, 0)

    for hs in range(2):

        @pl.when(jnp.logical_not(mine & (h == hs)))
        def _():
            pltpu.make_async_copy(fin.at[hs], fin.at[hs], f_r.at[hs]).wait()

    total = fin[0].astype(F32) + fin[1].astype(F32)
    left = lax.broadcasted_iota(jnp.int32, (32, WIDE), 1) < HEAD
    scale = jnp.where(left, SCALE, 1.0)
    dkv_out[:32] = (total[:, :WIDE] * scale).astype(BF16)
    dkv_out[32:] = (total[:, WIDE:] * scale).astype(BF16)
    for copy in sent:
        copy.wait_send()
    forward[1].wait_send()
    pl.when(jnp.logical_not(mine))(forward[0].wait_send)
    def ended(k, _):
        share(k).wait_send()

        pl.when(k < 7)(give(jnp.minimum(k, 6)).wait_send)
        return 0

    lax.fori_loop(0, 8, ended, 0)

    def rows_ended(i, _):
        for j in range(1, 4):
            row_ways(i, j).wait_send()
        pl.when(i > 0)(row_ways(i, 0).wait_send)
        return 0

    lax.fori_loop(0, 4, rows_ended, 0)


def per_device(query_matrix, key_matrix, value_matrix, output_gradient, stripe_map):
    vmem = pl.BlockSpec(memory_space=pltpu.VMEM)
    dma = pltpu.SemaphoreType.DMA
    dq, dkv = pl.pallas_call(
        kernel,
        out_shape=[
            jax.ShapeDtypeStruct((4, TOK, WIDE), BF16),
            jax.ShapeDtypeStruct((TOK, WIDE), BF16),
        ],
        in_specs=[pl.BlockSpec(memory_space=pltpu.SMEM)] + [vmem] * 4,
        out_specs=[vmem, vmem],
        scratch_shapes=[
            pltpu.VMEM((4, TOK, 2 * WIDE), BF16),
            pltpu.VMEM((4, 32, 2 * WIDE), BF16),
            pltpu.VMEM((4, 4, TOK, 2 * WIDE), BF16),
            pltpu.VMEM((2, 8, 4, 16, 2 * WIDE), BF16),
            pltpu.VMEM((8, RT, WIDE), BF16),
            pltpu.VMEM((8, HEAD, RT), BF16),
            pltpu.VMEM((8, RT, WIDE), BF16),
            pltpu.VMEM((8, RT, WIDE), BF16),
            pltpu.VMEM((8, 8, RT, RT), F32),
            pltpu.VMEM((8, 8, RT, RT), F32),
            pltpu.VMEM((8, 8, RT), F32),
            pltpu.VMEM((8, 8, RT), F32),
            pltpu.VMEM((8, 8, RT), F32),
            pltpu.VMEM((3, 8, RT), F32),
            pltpu.VMEM((4, 3, 8, RT), F32),
            pltpu.VMEM((8, 8, RT), F32),
            pltpu.VMEM((8, RT), F32),
            pltpu.VMEM((2, HEAD, RT), F32),
            pltpu.VMEM((RT, WIDE), F32),
            pltpu.VMEM((8, 2, 32, 2 * WIDE), F32),
            pltpu.VMEM((8, 2, 32, 2 * WIDE), BF16),
            pltpu.VMEM((8, 2, 32, 2 * WIDE), BF16),
            pltpu.VMEM((7, 2, 32, 2 * WIDE), BF16),
            pltpu.VMEM((7, 2, 32, 2 * WIDE), BF16),
            pltpu.VMEM((2, 32, 2 * WIDE), BF16),
            pltpu.VMEM((2, 32, 2 * WIDE), BF16),
            pltpu.VMEM((4, 4, 32, 2 * WIDE), BF16),
            pltpu.VMEM((4, 4, 32, 2 * WIDE), BF16),
            dma((2,)), dma((N_SEM,)), dma((N_SEM,)),
            dma((2,)), dma((2,)), dma((7,)), dma((7,)),
            dma((8,)), dma((8,)), dma((4, 4)), dma((4, 4)),
        ],
        compiler_params=pltpu.CompilerParams(
            collective_id=0, has_side_effects=True, vmem_limit_bytes=50 * 2**20
        ),
    )(
        stripe_map,
        query_matrix.transpose(1, 0, 2),
        output_gradient.transpose(1, 0, 2),
        key_matrix,
        value_matrix,
    )
    return dq.transpose(1, 0, 2), dkv[:, :HEAD], dkv[:, HEAD:]


def solution(mesh):
    return jax.shard_map(
        per_device,
        mesh=mesh,
        in_specs=(
            P(("blk", "uly"), None, "tp"),
            P(("blk", "uly"), None),
            P(("blk", "uly"), None),
            P(("blk", "uly"), None, "tp"),
            P(),
        ),
        out_specs=(P(("blk", "uly"), None, "tp"), P(("blk", "uly"), "tp"), P(("blk", "uly"), "tp")),
        check_vma=False,
    )
```
